32 devices in a mesh: dp: 16 (over z, y, x), tensor: 2 (over core).
Axes of the slice: x: 2, y: 2, z: 4, core: 2. Of those that a mesh axis runs over, the one named last changes fastest.
Arguments:
- inputs: bfloat16 [8192, 768], P(('dp', 'tensor')), may hold values from -6 to 6
- segments: int32 [8192], P('dp'), may hold values from 0 to 2, as said below
- gain_first: float32 [768], P(('dp', 'tensor')), may hold values from 0.5 to 1.5
- gain_second: float32 [768], P(('dp', 'tensor')), may hold values from 0.5 to 1.5
- attend_weight: bfloat16 [3, 768, 768], P(None, 'dp', 'tensor'), may hold values from -0.21875 to 0.21875
- mixing_matrix: bfloat16 [768, 768], P('dp', 'tensor'), may hold values from -0.875 to 0.875
- expand_matrix: bfloat16 [2, 768, 1152], P(None, 'dp', 'tensor'), may hold values from -0.21875 to 0.21875
- reduce_matrix: bfloat16 [768, 1152], P('dp', 'tensor'), may hold values from -0.1875 to 0.1875
- cotangent: bfloat16 [8192, 768], P(('dp', 'tensor')), may hold values from -6 to 6
Outputs:
- output: bfloat16 [8192, 768], P(('dp', 'tensor'))
- input_grad: float32 [8192, 768], P(('dp', 'tensor'))
- first_grad: float32 [768], P(('dp', 'tensor'))
- second_grad: float32 [768], P(('dp', 'tensor'))
- attend_grad: float32 [3, 768, 768], P(None, 'dp', 'tensor')
- mixing_grad: float32 [768, 768], P('dp', 'tensor')
- expand_grad: float32 [2, 768, 1152], P(None, 'dp', 'tensor')
- reduce_grad: float32 [768, 1152], P('dp', 'tensor')
The draws below stay inside these ranges and needn't reach their ends.
Inputs may be any that keep to these rules, and one draw needn't show every extreme that they name: `segments`: in each aligned block of 512 tokens (one sequence) the numbers start at 0, never fall and rise by one at two places, so each sequence holds three documents of 128 tokens or more; the middle one covers positions 255 and 256 of its sequence.
All inputs are finite; a program needn't handle non-finite values.
Results may differ from the reference program's by a relative error of at most 0.018.
Values may be sent and summed in bfloat16 or wider, within the bound.
A program may use at most 128 MiB of HBM per device.

```python
import math
import jax
import jax.numpy as jnp
from jax import lax

D = 768
HEAD_SIZE = 64
FF = 1152
SEQ_LEN = 512
SEQS = 16
TOKENS = 8192


def draw_segments(key, part):
    key = jax.random.fold_in(key, 7)
    key_one, key_two = jax.random.split(key, 2)
    shape_cut = (SEQS, 1)
    cut_first = jax.random.randint(key_one, shape_cut, SEQ_LEN // 4, 3 * SEQ_LEN // 8 + 1)
    cut_second = jax.random.randint(key_two, shape_cut, 5 * SEQ_LEN // 8, 3 * SEQ_LEN // 4 + 1)
    positions = jnp.arange(SEQ_LEN, dtype=jnp.int32)[None, :]
    numbers = (positions >= cut_first).astype(jnp.int32) + (positions >= cut_second).astype(jnp.int32)
    return numbers.reshape(SEQS * SEQ_LEN).astype(jnp.int32)


def with_spikes(values, rng, source, target, parts, factor):
    owner, partner = [(jnp.arange(values.shape[position]) // (values.shape[position] // parts)).reshape([-1 if axis == position else 1 for axis in range(values.ndim)]) for position in (source, target)]
    chosen = jax.random.permutation(rng, parts)[partner]
    strong = (owner == chosen) | (owner == (partner + parts // 2) % parts)
    return jnp.where(strong, factor * values, values)


def block_scale(own_key, extent, cuts, low, high):
    def one(position, shards_of):
        draws = jax.random.uniform(jax.random.fold_in(jax.random.fold_in(own_key, 6), position), (shards_of,), jnp.float32, low / len(cuts), high / len(cuts))
        return jnp.repeat(jnp.exp(draws), extent[position] // shards_of).reshape((-1,) + (1,) * (len(extent) - position - 1))

    loudness = one(*cuts[0])
    for cut in cuts[1:]:
        loudness = loudness * one(*cut)
    return loudness


def bell_draw(key, extent, width, most, pieces=(), kind=jnp.bfloat16):
    entries = jax.random.normal(key, extent, jnp.float32) * width
    if len(pieces) > 0:
        entries = block_scale(key, extent, pieces, -0.22, 0.18) * entries
    return jnp.clip(entries, min=-most, max=most).astype(kind)


def noise_with(own_key, shape, spread, bound, cuts, heavy, held_as=jnp.bfloat16):
    values = spread * jax.random.normal(own_key, shape, jnp.float32)
    if cuts:
        values = values * block_scale(own_key, shape, cuts, -0.22, 0.18)
    return jnp.clip(with_spikes(values, jax.random.fold_in(own_key, 3), *heavy), -bound, bound).astype(held_as)


def setup_inputs(seed: int = 0) -> dict:
    keys = jax.random.split(jax.random.key(seed), 10)
    inputs = noise_with(keys[0], (TOKENS, D), 1.0, 6.0, ((0, 32),), (0, 1, 32, 2.75))
    segments = draw_segments(jax.random.fold_in(keys[9], 71), 0)
    gain_first = jnp.clip(1.0 + 0.1 * jax.random.normal(keys[2], (D,), jnp.float32), 0.5, 1.5)
    gain_second = jnp.clip(1.0 + 0.1 * jax.random.normal(keys[3], (D,), jnp.float32), 0.5, 1.5)
    attend_weight = bell_draw(keys[4], (3, D, D), D ** -0.5, 0.21875, ((1, 16), (2, 2)))
    mixing_matrix = bell_draw(keys[5], (D, D), (D // 16) ** -0.5, 0.875, ((0, 16), (1, 2)))
    expand_matrix = bell_draw(keys[6], (2, D, FF), D ** -0.5, 0.21875, ((1, 16), (2, 2)))
    reduce_matrix = bell_draw(keys[7], (D, FF), FF ** -0.5, 0.1875, ((0, 16), (1, 2)))
    cotangent = noise_with(keys[8], (TOKENS, D), 1.0, 6.0, ((0, 32),), (0, 1, 32, 2.75))
    return dict(inputs=inputs, segments=segments, gain_first=gain_first, gain_second=gain_second, attend_weight=attend_weight, mixing_matrix=mixing_matrix, expand_matrix=expand_matrix, reduce_matrix=reduce_matrix, cotangent=cotangent)


EPS = 1e-05
THETA = 160000.0
MASKED = -1e+30
FULL_PRECISION = lax.Precision.HIGHEST

@jax.custom_vjp
def low(v):
    return lax.optimization_barrier(v.astype(jnp.bfloat16)).astype(jnp.float32)

@jax.custom_vjp
def reduced_backward(v):
    return v

def low_keep(v):
    return (low(v), None)

def low_pass(kept, grad):
    return (grad,)

def back_keep(v):
    return (v, None)

def back_low(kept, grad):
    return (low(grad),)
low.defvjp(low_keep, low_pass)
reduced_backward.defvjp(back_keep, back_low)

def rotary_tables(length, head_size):
    indices = jnp.arange(head_size // 2, dtype=jnp.float32)
    inverse_freq = THETA ** (-(2.0 / head_size) * indices)
    angles = jnp.arange(length, dtype=jnp.float32)[:, None] * inverse_freq[None, :]
    angles = jnp.concatenate([angles, angles], axis=1)
    return (jnp.cos(angles), jnp.sin(angles))

def rotate_half(values):
    midway = values.shape[-1] // 2
    return jnp.concatenate([-values[..., midway:], values[..., :midway]], axis=-1)

def layer_norm(values):
    centered = values - lax.optimization_barrier(jnp.mean(values, axis=-1, keepdims=True))
    return centered * lax.rsqrt(lax.optimization_barrier(jnp.mean(centered * centered, axis=-1, keepdims=True)) + EPS)

def block_forward(block_rows, block_segments, weights_all):
    gain_first, gain_second, attend_weight, mixing_matrix, expand_matrix, reduce_matrix = weights_all
    seq_count, length, model_width = block_rows.shape
    head_count = model_width // HEAD_SIZE
    score_scale = HEAD_SIZE ** (-0.5)
    cosine_table, sine_table = rotary_tables(length, HEAD_SIZE)
    cosine_table = cosine_table[None, :, None, :]
    sine_table = sine_table[None, :, None, :]
    first_normed = low(layer_norm(block_rows) * gain_first)

    def project(weight_matrix):
        gated_product = jnp.einsum('ryi,ic->ryc', first_normed, weight_matrix, precision=FULL_PRECISION)
        return gated_product.reshape(seq_count, length, head_count, HEAD_SIZE)
    query_raw = reduced_backward(project(attend_weight[0]))
    key_raw = reduced_backward(project(attend_weight[1]))
    value_raw = reduced_backward(project(attend_weight[2]))
    query_heads = low((query_raw * cosine_table + rotate_half(query_raw) * sine_table) * score_scale)
    key_heads = low(key_raw * cosine_table + rotate_half(key_raw) * sine_table)
    value_heads = low(value_raw)
    scores = reduced_backward(jnp.einsum('sqhd,skhd->shqk', query_heads, key_heads, precision=FULL_PRECISION))
    same_doc = (block_segments[:, :, None] == block_segments[:, None, :])[:, None, :, :]
    softmax_out = jax.nn.softmax(jnp.where(same_doc, scores, MASKED), axis=-1)
    mixed_heads = jnp.einsum('shqk,skhd->sqhd', low(softmax_out), value_heads, precision=FULL_PRECISION)
    attended_rows = low(reduced_backward(mixed_heads)).reshape(seq_count, length, model_width)
    branch_output = reduced_backward(jnp.einsum('vjo,io->vji', attended_rows, mixing_matrix, precision=FULL_PRECISION))
    middle = block_rows + branch_output
    second_normed = low(layer_norm(middle) * gain_second)
    activated_input = reduced_backward(jnp.einsum('qvh,hk->qvk', second_normed, expand_matrix[0], precision=FULL_PRECISION))
    gate_projected = reduced_backward(jnp.einsum('qvh,hk->qvk', second_normed, expand_matrix[1], precision=FULL_PRECISION))
    hidden_rows = low(jax.nn.gelu(activated_input, approximate=False) * gate_projected)
    second_branch = reduced_backward(jnp.einsum('xyt,nt->xyn', hidden_rows, reduce_matrix, precision=FULL_PRECISION))
    return middle + second_branch

def reference(inputs, segments, gain_first, gain_second, attend_weight, mixing_matrix, expand_matrix, reduce_matrix, cotangent):
    per_scan = math.gcd(SEQS, max(1, 4096 // SEQ_LEN))
    blocks = SEQS // per_scan
    segment_blocks = segments.reshape(blocks, per_scan, SEQ_LEN)
    checked = jax.checkpoint(block_forward)

    def forward(rows_in, *weights_all):
        grouped = rows_in.reshape(blocks, per_scan, SEQ_LEN, D)

        def scan_step(carried, per_block):
            return (carried, checked(per_block[0], per_block[1], weights_all))
        unused, result = lax.scan(scan_step, jnp.zeros((), jnp.float32), (grouped, segment_blocks))
        return result.reshape(TOKENS, D)
    primals = (inputs.astype(jnp.float32), gain_first.astype(jnp.float32), gain_second.astype(jnp.float32), attend_weight.astype(jnp.float32), mixing_matrix.astype(jnp.float32), expand_matrix.astype(jnp.float32), reduce_matrix.astype(jnp.float32))
    output, pullback = jax.vjp(forward, *primals)
    gradients = pullback(cotangent.astype(jnp.float32))
    return (output.astype(jnp.bfloat16), gradients[0], gradients[1], gradients[2], gradients[3], gradients[4], gradients[5], gradients[6])
```

```python
import functools
import math

import jax
import jax.numpy as jnp
from jax import lax
from jax.experimental import pallas as pl
from jax.experimental.pallas import tpu as pltpu
from jax.sharding import PartitionSpec as P

HEAD_SIZE = 64
EPS = 1e-05
THETA = 160000.0
MASKED = -1e30
LANES = 128
VMEM_LIMIT = 60 * 1024 * 1024
MESH = pl.DeviceIdType.MESH
VMEM = pltpu.VMEM


def normalize(values):
    centered = values - jnp.mean(values, axis=-1, keepdims=True)
    inverse_std = lax.rsqrt(jnp.mean(centered * centered, axis=-1, keepdims=True) + EPS)
    return (centered * inverse_std, inverse_std)


def normalize_back(grad_unit, unit_rows, inverse_std):
    plain_mean = jnp.mean(grad_unit, axis=-1, keepdims=True)
    cross_mean = jnp.mean(grad_unit * unit_rows, axis=-1, keepdims=True)
    return inverse_std * (grad_unit - plain_mean - unit_rows * cross_mean)


def plain(left_side, right_side):
    return jnp.dot(left_side, right_side, preferred_element_type=jnp.float32)


def contract_last(left_side, right_side):
    return lax.dot_general(
        left_side, right_side, (((1,), (1,)), ((), ())), preferred_element_type=jnp.float32
    )


def contract_first(left_side, right_side):
    return lax.dot_general(
        left_side, right_side, (((0,), (0,)), ((), ())), preferred_element_type=jnp.float32
    )


def gelu_slope(values):
    return 0.5 * (1.0 + lax.erf(values / math.sqrt(2.0))) + values * jnp.exp(
        -0.5 * values * values
    ) / math.sqrt(2.0 * math.pi)


def position():
    dp, core = lax.axis_index("dp"), lax.axis_index("tensor")
    zh, zl = lax.rem(lax.div(dp, 8), 2), lax.rem(lax.div(dp, 4), 2)
    y, x = lax.rem(lax.div(dp, 2), 2), lax.rem(dp, 2)
    peers = dict(
        core=(dp, 1 - core),
        x=(dp + 1 - 2 * x, core),
        y=(dp + 2 - 4 * y, core),
        zl=(dp + 4 - 8 * zl, core),
        zh=(dp + 8 - 16 * zh, core),
    )
    return core, zh, zl, y, x, peers


def greet(peers):
    barrier = pltpu.get_barrier_semaphore()
    for peer in peers.values():
        pl.semaphore_signal(barrier, inc=1, device_id=peer, device_id_type=MESH)
    pl.semaphore_wait(barrier, len(peers))


def gather_kernel(chunks, *refs):
    kinds = 1 + max(kind for kind, _ in chunks)
    shards, tokens = refs[:kinds], refs[kinds]
    fulls, other_tokens = refs[kinds + 1 : 2 * kinds + 1], refs[2 * kinds + 1]
    own_sem, send_sem, recv_sem, token_sem = refs[2 * kinds + 2 :]
    core, zh, zl, y, x, peers = position()
    every = slice(None)

    def remote(k, slot, source, target, peer):
        return pltpu.make_async_remote_copy(
            src_ref=source,
            dst_ref=target,
            send_sem=send_sem.at[k, slot],
            recv_sem=recv_sem.at[k, slot],
            device_id=peers[peer],
            device_id_type=MESH,
        )

    def same(k, slot, index, peer):
        kind, j = chunks[k]
        block = fulls[kind].at[(core, j) + index]
        return remote(k, slot, block, block, peer)

    own = []
    for k, (kind, j) in enumerate(chunks):
        own.append(
            pltpu.make_async_copy(
                shards[kind].at[j], fulls[kind].at[core, j, zh, zl, y, x], own_sem.at[k]
            )
        )
    stages = [[] for _ in chunks]
    for k, (kind, j) in enumerate(chunks):
        stages[k] = [
            [
                remote(
                    k, 0, shards[kind].at[j], fulls[kind].at[core, j, zh, zl, y, x], "zh"
                )
            ],
            [same(k, 1, (every, zl, y, x), "zl")],
            [same(k, 2, (every, 0, y, x), "x"), same(k, 3, (every, 1, y, x), "y")],
            [same(k, 4, (every, 0, y), "y"), same(k, 5, (every, 1, every, x), "x")],
            [same(k, 6, (), "core")],
        ]
    token_copy = pltpu.make_async_remote_copy(
        src_ref=tokens,
        dst_ref=other_tokens,
        send_sem=token_sem.at[0],
        recv_sem=token_sem.at[1],
        device_id=peers["core"],
        device_id_type=MESH,
    )
    for copy in own:
        copy.start()
    greet(peers)
    token_copy.start()
    count, depth = len(chunks), 5
    for step in range(count + depth):
        for stage in range(depth, -1, -1):
            k = step - stage
            if 0 <= k < count:
                if stage > 0:
                    for copy in stages[k][stage - 1]:
                        copy.wait_recv()
                if stage == 1:
                    own[k].wait()
                if stage < depth:
                    for copy in stages[k][stage]:
                        copy.start()
    for per_chunk in stages:
        for group in per_chunk:
            for copy in group:
                copy.wait_send()
    token_copy.wait()


def gather_all(shards, chunks, tokens):
    blocks = [
        jax.ShapeDtypeStruct((2, s.shape[0], 2, 2, 2, 2) + s.shape[1:], s.dtype) for s in shards
    ]
    anywhere = pl.BlockSpec(memory_space=pl.ANY)
    count = len(chunks)
    out = pl.pallas_call(
        functools.partial(gather_kernel, chunks),
        out_shape=blocks + [jax.ShapeDtypeStruct(tokens.shape, tokens.dtype)],
        in_specs=[anywhere] * (len(shards) + 1),
        out_specs=[anywhere] * (len(shards) + 1),
        scratch_shapes=[
            pltpu.SemaphoreType.DMA((count,)),
            pltpu.SemaphoreType.DMA((count, 7)),
            pltpu.SemaphoreType.DMA((count, 7)),
            pltpu.SemaphoreType.DMA((2,)),
        ],
        compiler_params=pltpu.CompilerParams(
            collective_id=0, has_side_effects=True, vmem_limit_bytes=VMEM_LIMIT
        ),
    )(*shards, tokens)
    fulls = [
        full.reshape((2, s.shape[0], 16 * s.shape[1], s.shape[2]))
        for full, s in zip(out[:-1], shards)
    ]
    return fulls, out[-1]


def reduce_kernel(chunks, kinds, *refs):
    parts, rows = refs[:kinds], refs[kinds]
    outs, other_rows = refs[kinds + 1 : 2 * kinds + 1], refs[2 * kinds + 1]
    refs = refs[2 * kinds + 2 :]
    sums, firsts, seconds, thirds, fourths = (
        refs[i * kinds : (i + 1) * kinds] for i in range(5)
    )
    send_sem, recv_sem, row_sem = refs[5 * kinds :]
    core, zh, zl, y, x, peers = position()
    every = slice(None)

    def remote(k, slot, source, target, peer):
        return pltpu.make_async_remote_copy(
            src_ref=source,
            dst_ref=target,
            send_sem=send_sem.at[k, slot],
            recv_sem=recv_sem.at[k, slot],
            device_id=peers[peer],
            device_id_type=MESH,
        )

    stages = []
    for k, (kind, j) in enumerate(chunks):
        part, total = parts[kind], sums[kind].at[j]
        stages.append(
            [
                [remote(k, 0, part.at[1 - core, j], total, "core")],
                [
                    remote(k, 1, total.at[every, 0, every, 1 - x], firsts[kind].at[j, 0], "x"),
                    remote(k, 2, total.at[every, 1, 1 - y], firsts[kind].at[j, 1], "y"),
                ],
                [
                    remote(k, 3, total.at[every, 0, 1 - y, x], seconds[kind].at[j, 0], "y"),
                    remote(k, 4, total.at[every, 1, y, 1 - x], seconds[kind].at[j, 1], "x"),
                ],
                [remote(k, 5, total.at[every, 1 - zl, y, x], thirds[kind].at[j], "zl")],
                [remote(k, 6, total.at[1 - zh, zl, y, x], fourths[kind].at[j], "zh")],
            ]
        )

    def add(k, stage):
        kind, j = chunks[k]
        part, total = parts[kind], sums[kind]
        if stage == 0:

            @pl.loop(0, 16)
            def _(b):
                at = (lax.div(b, 8), lax.rem(lax.div(b, 4), 2), lax.rem(lax.div(b, 2), 2), lax.rem(b, 2))
                total[(j,) + at] = total[(j,) + at] + part[(core, j) + at]

        elif stage == 1:

            @pl.loop(0, 4)
            def _(b):
                hi, lo = lax.div(b, 2), lax.rem(b, 2)
                total[j, hi, 0, lo, x] = total[j, hi, 0, lo, x] + firsts[kind][j, 0, hi, lo]
                total[j, hi, 1, y, lo] = total[j, hi, 1, y, lo] + firsts[kind][j, 1, hi, lo]

        elif stage == 2:

            @pl.loop(0, 2)
            def _(hi):
                total[j, hi, 0, y, x] = total[j, hi, 0, y, x] + seconds[kind][j, 0, hi]
                total[j, hi, 1, y, x] = total[j, hi, 1, y, x] + seconds[kind][j, 1, hi]

        elif stage == 3:

            @pl.loop(0, 2)
            def _(hi):
                total[j, hi, zl, y, x] = total[j, hi, zl, y, x] + thirds[kind][j, hi]

        else:
            outs[kind][j] = total[j, zh, zl, y, x].astype(jnp.float32) + fourths[kind][
                j
            ].astype(jnp.float32)

    row_copy = pltpu.make_async_remote_copy(
        src_ref=rows,
        dst_ref=other_rows,
        send_sem=row_sem.at[0],
        recv_sem=row_sem.at[1],
        device_id=peers["core"],
        device_id_type=MESH,
    )
    greet(peers)
    count, depth = len(chunks), 5
    for step in range(count + depth):
        for stage in range(depth, -1, -1):
            k = step - stage
            if 0 <= k < count:
                if stage > 0:
                    for copy in stages[k][stage - 1]:
                        copy.wait_recv()
                    add(k, stage - 1)
                if stage < depth:
                    for copy in stages[k][stage]:
                        copy.start()
        if step == count - 1:
            row_copy.start()
    for per_chunk in stages:
        for group in per_chunk:
            for copy in group:
                copy.wait_send()
    row_copy.wait()


def reduce_all(parts, chunks, rows):
    parts = [
        part.reshape(part.shape[:2] + (2, 2, 2, 2, part.shape[2] // 16, part.shape[3]))
        for part in parts
    ]
    kinds, count = len(parts), len(chunks)
    whole = pl.BlockSpec(memory_space=VMEM)

    def buffers(dims):
        return [VMEM((p.shape[1],) + dims + p.shape[-2:], p.dtype) for p in parts]

    out = pl.pallas_call(
        functools.partial(reduce_kernel, chunks, kinds),
        out_shape=[
            jax.ShapeDtypeStruct((p.shape[1],) + p.shape[-2:], jnp.float32) for p in parts
        ]
        + [jax.ShapeDtypeStruct(rows.shape, rows.dtype)],
        in_specs=[whole] * (kinds + 1),
        out_specs=[whole] * (kinds + 1),
        scratch_shapes=buffers((2, 2, 2, 2))
        + buffers((2, 2, 2))
        + buffers((2, 2))
        + buffers((2,))
        + buffers(())
        + [
            pltpu.SemaphoreType.DMA((count, 7)),
            pltpu.SemaphoreType.DMA((count, 7)),
            pltpu.SemaphoreType.DMA((2,)),
        ],
        compiler_params=pltpu.CompilerParams(
            collective_id=1, has_side_effects=True, vmem_limit_bytes=VMEM_LIMIT
        ),
    )(*parts, rows)
    return out[:-1], out[-1]


def half_turn(values):
    lane = lax.broadcasted_iota(jnp.int32, values.shape, 1)
    low = lax.rem(lane, HEAD_SIZE) < HEAD_SIZE // 2
    shift = HEAD_SIZE // 2
    return jnp.where(
        low, -pltpu.roll(values, LANES - shift, 1), pltpu.roll(values, shift, 1)
    )


def attend_kernel(
    normed, wq, wk, wv, cosine, sine, seg_rows, seg_cols, q_out, k_out, v_out, att_out, log_out
):
    own = q_out.shape[0]
    cos, sin = cosine[...], sine[...]
    query = plain(normed[:own], wq[0, 0])
    query = query * cos[:own] + half_turn(query) * sin[:own]
    query = (query * HEAD_SIZE**-0.5).astype(jnp.bfloat16)
    keys = plain(normed[...], wk[0, 0])
    keys = (keys * cos + half_turn(keys) * sin).astype(jnp.bfloat16)
    value = plain(normed[...], wv[0, 0]).astype(jnp.bfloat16)
    q_out[...], k_out[...], v_out[...] = query, keys, value
    allowed = seg_rows[...] == seg_cols[...]
    mixed, logs = [], []
    for head in range(LANES // HEAD_SIZE):
        part = slice(head * HEAD_SIZE, (head + 1) * HEAD_SIZE)
        scores = jnp.where(allowed, contract_last(query[:, part], keys[:, part]), MASKED)
        peak = jnp.max(scores, axis=-1, keepdims=True)
        exponent = jnp.exp(scores - peak)
        total = jnp.sum(exponent, axis=-1, keepdims=True)
        probs = (exponent / total).astype(jnp.bfloat16)
        mixed.append(plain(probs, value[:, part]).astype(jnp.bfloat16))
        logs.append(jnp.broadcast_to(peak + jnp.log(total), (own, HEAD_SIZE)))
    att_out[...] = jnp.concatenate(mixed, axis=1)
    log_out[...] = jnp.concatenate(logs, axis=1)


def attend_back_kernel(
    normed, branch, wq, wk, wv, mix, cosine, sine, seg_rows, seg_cols, q_in, k_in, v_in, att_in,
    log_in, weight_out, mix_out, normed_out,
):
    own = q_in.shape[0]
    step = pl.program_id(0)
    cos, sin = cosine[...], sine[...]
    query, keys, value = q_in[...], k_in[...], v_in[...]
    grad = plain(branch[...], mix[0, 0]).astype(jnp.bfloat16)
    allowed = seg_rows[...] == seg_cols[...]
    grad_q, grad_k, grad_v = [], [], []
    for head in range(LANES // HEAD_SIZE):
        part = slice(head * HEAD_SIZE, (head + 1) * HEAD_SIZE)
        qh, kh, vh, gh = query[:, part], keys[:, part], value[:, part], grad[:, part]
        log_total = log_in[:, head * HEAD_SIZE : head * HEAD_SIZE + 1]
        scores = jnp.where(allowed, contract_last(qh, kh), MASKED)
        probs = jnp.exp(scores - log_total)
        grad_v.append(contract_first(probs.astype(jnp.bfloat16), gh))
        grad_probs = contract_last(gh, vh)
        inner = jnp.sum(grad_probs * probs, axis=-1, keepdims=True)
        grad_scores = (probs * (grad_probs - inner)).astype(jnp.bfloat16)
        grad_q.append(plain(grad_scores, kh))
        grad_k.append(contract_first(grad_scores, qh))
    gq = jnp.concatenate(grad_q, axis=1) * HEAD_SIZE**-0.5
    gk = jnp.concatenate(grad_k, axis=1)
    gv = jnp.concatenate(grad_v, axis=1).astype(jnp.bfloat16)
    gq = (gq * cos[:own] - half_turn(gq * sin[:own])).astype(jnp.bfloat16)
    gk = (gk * cos - half_turn(gk * sin)).astype(jnp.bfloat16)
    weight_out[0, 0] = contract_first(normed[:own], gq).astype(jnp.bfloat16)
    weight_out[0, 1] = contract_first(normed[...], gk).astype(jnp.bfloat16)
    weight_out[0, 2] = contract_first(normed[...], gv).astype(jnp.bfloat16)
    mix_out[0, 0] = contract_first(branch[...], att_in[...]).astype(jnp.bfloat16)
    update = contract_last(gk, wk[0, 0]) + contract_last(gv, wv[0, 0])
    first = contract_last(gq, wq[0, 0])

    @pl.when(step == 0)
    def _():
        normed_out[...] = update

    @pl.when(step > 0)
    def _():
        normed_out[...] += update

    normed_out[:own] += first


def attention_specs(width, own, length, groups):
    def weight(j):
        return pl.BlockSpec((1, 1, width, LANES), lambda p: (p // groups, j, 0, p % groups))

    def columns(rows):
        return pl.BlockSpec((rows, LANES), lambda p: (0, p))

    def whole(*shape):
        return pl.BlockSpec(shape, lambda p: (0,) * len(shape))

    return weight, columns, whole


def attend(normed, weights, cosine, sine, seg_rows, seg_cols):
    length, width = normed.shape
    own = seg_rows.shape[0]
    groups = weights.shape[3] // LANES
    weight, columns, whole = attention_specs(width, own, length, groups)
    heads = 2 * groups * LANES
    return pl.pallas_call(
        attend_kernel,
        grid=(2 * groups,),
        out_shape=[
            jax.ShapeDtypeStruct((own, heads), jnp.bfloat16),
            jax.ShapeDtypeStruct((length, heads), jnp.bfloat16),
            jax.ShapeDtypeStruct((length, heads), jnp.bfloat16),
            jax.ShapeDtypeStruct((own, heads), jnp.bfloat16),
            jax.ShapeDtypeStruct((own, heads), jnp.float32),
        ],
        in_specs=[
            whole(length, width), weight(0), weight(1), weight(2), whole(length, LANES),
            whole(length, LANES), whole(own, 1), whole(1, length),
        ],
        out_specs=[columns(own), columns(length), columns(length), columns(own), columns(own)],
        compiler_params=pltpu.CompilerParams(vmem_limit_bytes=VMEM_LIMIT),
    )(normed, weights, weights, weights, cosine, sine, seg_rows, seg_cols)


def attend_back(normed, branch, weights, mixing, cosine, sine, seg_rows, seg_cols, saved):
    length, width = normed.shape
    own = seg_rows.shape[0]
    groups = weights.shape[3] // LANES
    weight, columns, whole = attention_specs(width, own, length, groups)
    return pl.pallas_call(
        attend_back_kernel,
        grid=(2 * groups,),
        out_shape=[
            jax.ShapeDtypeStruct((2, 3, width, groups * LANES), jnp.bfloat16),
            jax.ShapeDtypeStruct((2, 1, width, groups * LANES), jnp.bfloat16),
            jax.ShapeDtypeStruct((length, width), jnp.float32),
        ],
        in_specs=[
            whole(length, width), whole(own, width), weight(0), weight(1), weight(2), weight(0),
            whole(length, LANES), whole(length, LANES), whole(own, 1), whole(1, length),
            columns(own), columns(length), columns(length), columns(own), columns(own),
        ],
        out_specs=[
            pl.BlockSpec((1, 3, width, LANES), lambda p: (p // groups, 0, 0, p % groups)),
            weight(0),
            whole(length, width),
        ],
        compiler_params=pltpu.CompilerParams(vmem_limit_bytes=VMEM_LIMIT),
    )(normed, branch, weights, weights, weights, mixing, cosine, sine, seg_rows, seg_cols, *saved)


def rotary_tables(length, core):
    indices = jnp.arange(HEAD_SIZE // 2, dtype=jnp.float32)
    inverse_freq = THETA ** (-(2.0 / HEAD_SIZE) * indices)
    angles = jnp.arange(length, dtype=jnp.float32)[:, None] * inverse_freq[None, :]
    angles = jnp.tile(angles, (1, LANES // (HEAD_SIZE // 2)))
    return own_first(jnp.cos(angles), core), own_first(jnp.sin(angles), core)


def own_first(rows, core):
    return jnp.where(core == 0, rows, jnp.roll(rows, rows.shape[0] // 2, axis=0))


def per_device(
    doubling,
    inputs,
    segments,
    gain_first,
    gain_second,
    attend_weight,
    mixing_matrix,
    expand_matrix,
    reduce_matrix,
    cotangent,
):
    core = lax.axis_index("tensor")
    own, width = inputs.shape
    length = segments.shape[0]
    share = gain_first.shape[0]
    shards = [attend_weight, mixing_matrix[None], expand_matrix, reduce_matrix[None]]
    if doubling:
        gains = jnp.zeros((1, 8, LANES), jnp.float32)
        gains = gains.at[0, 0, :share].set(gain_first).at[0, 1, :share].set(gain_second)
        order = ((4, 0), (0, 0), (0, 1), (0, 2), (1, 0), (2, 0), (2, 1), (3, 0))
        fulls, other_inputs = gather_all(shards + [gains], order, inputs)
        attend_full, mixing_full, expand_full, reduce_full, gains = fulls
        gains = gains.reshape(2, -1, 8, LANES)[:, :, :2, :share]
        full_first, full_second = jnp.transpose(gains, (2, 1, 0, 3)).reshape(2, width)
    else:
        both = ("dp", "tensor")
        full_first = lax.all_gather(gain_first, both, axis=0, tiled=True)
        full_second = lax.all_gather(gain_second, both, axis=0, tiled=True)
        attend_full, mixing_full, expand_full, reduce_full = (
            lax.all_gather(lax.all_gather(s, "dp", axis=1, tiled=True), "tensor", axis=0)
            for s in shards
        )
        pair = lax.all_gather(inputs, "tensor", axis=0)
        other_inputs = jnp.where(core == 0, pair[1], pair[0])

    cosine, sine = rotary_tables(length, core)
    segments = own_first(segments, core)
    seg_rows, seg_cols = segments[:own, None], segments[None, :]

    rows_all = jnp.concatenate([inputs, other_inputs]).astype(jnp.float32)
    rows_in = rows_all[:own]
    unit_one, inverse_one = normalize(rows_all)
    normed_one = (unit_one * full_first).astype(jnp.bfloat16)
    saved = attend(normed_one, attend_full, cosine, sine, seg_rows, seg_cols)
    attended = saved[3]
    half = attended.shape[1] // 2
    middle = (
        rows_in
        + contract_last(attended[:, :half], mixing_full[0, 0])
        + contract_last(attended[:, half:], mixing_full[1, 0])
    )
    unit_two, inverse_two = normalize(middle)
    normed_two = (unit_two * full_second).astype(jnp.bfloat16)
    output = middle
    grad_normed_two = jnp.zeros_like(middle)
    grad_expand, grad_reduce = [], []
    for side in range(2):
        activated_in = plain(normed_two, expand_full[side, 0])
        gate_linear = plain(normed_two, expand_full[side, 1])
        gelu_value = jax.nn.gelu(activated_in, approximate=False)
        hidden = (gelu_value * gate_linear).astype(jnp.bfloat16)
        output = output + contract_last(hidden, reduce_full[side, 0])
        grad_hidden = plain(cotangent, reduce_full[side, 0])
        grad_reduce.append(contract_first(cotangent, hidden).astype(jnp.bfloat16))
        grad_activated = (grad_hidden * gate_linear * gelu_slope(activated_in)).astype(
            jnp.bfloat16
        )
        grad_gate = (grad_hidden * gelu_value).astype(jnp.bfloat16)
        grad_expand.append(contract_first(normed_two, grad_activated).astype(jnp.bfloat16))
        grad_expand.append(contract_first(normed_two, grad_gate).astype(jnp.bfloat16))
        grad_normed_two = (
            grad_normed_two
            + contract_last(grad_activated, expand_full[side, 0])
            + contract_last(grad_gate, expand_full[side, 1])
        )
    hidden_width = expand_full.shape[3]
    grad_expand = jnp.stack(grad_expand).reshape(2, 2, width, hidden_width)
    grad_reduce = jnp.stack(grad_reduce).reshape(2, 1, width, hidden_width)
    second_local = jnp.sum(grad_normed_two * unit_two, axis=0)
    grad_middle = cotangent.astype(jnp.float32) + normalize_back(
        grad_normed_two * full_second, unit_two, inverse_two
    )
    grad_branch = grad_middle.astype(jnp.bfloat16)
    grad_attend, grad_mixing, grad_normed_one = attend_back(
        normed_one, grad_branch, attend_full, mixing_full, cosine, sine, seg_rows, seg_cols, saved
    )
    first_local = jnp.sum(grad_normed_one * unit_one, axis=0)
    through = normalize_back(grad_normed_one * full_first, unit_one, inverse_one)
    rows_mine = grad_middle + through[:own]
    rows_other = through[own:].astype(jnp.bfloat16)
    if doubling:
        local = jnp.stack([first_local, second_local]).reshape(2, -1, 2, share)
        local = jnp.transpose(local, (2, 1, 0, 3))
        local = jnp.pad(local, ((0, 0), (0, 0), (0, 6), (0, LANES - share)))
        local = local.reshape(2, 1, -1, LANES)
        order = ((3, 0), (2, 0), (2, 1), (0, 0), (0, 1), (0, 2), (1, 0), (4, 0))
        sent, rows_back = reduce_all(
            [grad_attend, grad_mixing, grad_expand, grad_reduce, local], order, rows_other
        )
        sent_attend, sent_mixing, sent_expand, sent_reduce, gains = sent
        sent_mixing, sent_reduce = sent_mixing[0], sent_reduce[0]
        first_grad, second_grad = gains[0, 0, :share], gains[0, 1, :share]
    else:

        def summed(part):
            part = part.astype(jnp.float32)
            part = lax.psum_scatter(part, "tensor", scatter_dimension=0, tiled=False)
            return lax.psum_scatter(part, "dp", scatter_dimension=1, tiled=True)

        sent_attend, sent_expand = summed(grad_attend), summed(grad_expand)
        sent_mixing, sent_reduce = summed(grad_mixing)[0], summed(grad_reduce)[0]
        first_grad, second_grad = (
            lax.psum_scatter(part, ("dp", "tensor"), scatter_dimension=0, tiled=True)
            for part in (first_local, second_local)
        )
        pair = lax.all_gather(rows_other, "tensor", axis=0)
        rows_back = jnp.where(core == 0, pair[1], pair[0])
    input_grad = rows_mine + rows_back.astype(jnp.float32)
    return (
        output.astype(jnp.bfloat16),
        input_grad,
        first_grad,
        second_grad,
        sent_attend,
        sent_mixing,
        sent_expand,
        sent_reduce,
    )


def solution(mesh):
    in_specs = (
        P(("dp", "tensor"), None),
        P("dp"),
        P(("dp", "tensor")),
        P(("dp", "tensor")),
        P(None, "dp", "tensor"),
        P("dp", "tensor"),
        P(None, "dp", "tensor"),
        P("dp", "tensor"),
        P(("dp", "tensor"), None),
    )
    out_specs = (
        P(("dp", "tensor"), None),
        P(("dp", "tensor"), None),
        P(("dp", "tensor")),
        P(("dp", "tensor")),
        P(None, "dp", "tensor"),
        P("dp", "tensor"),
        P(None, "dp", "tensor"),
        P("dp", "tensor"),
    )
    doubling = mesh.shape["dp"] == 16 and mesh.shape["tensor"] == 2
    return jax.shard_map(
        functools.partial(per_device, doubling),
        mesh=mesh,
        in_specs=in_specs,
        out_specs=out_specs,
        check_vma=False,
    )
```

```python
import functools
import math

import jax
import jax.numpy as jnp
from jax import lax
from jax.experimental import pallas as pl
from jax.experimental.pallas import tpu as pltpu
from jax.sharding import PartitionSpec as P

HEAD_SIZE = 64
EPS = 1e-05
THETA = 160000.0
MASKED = -1e30
LANES = 128
VMEM_LIMIT = 60 * 1024 * 1024
MESH = pl.DeviceIdType.MESH
VMEM = pltpu.VMEM


def normalize(values):
    centered = values - jnp.mean(values, axis=-1, keepdims=True)
    inverse_std = lax.rsqrt(jnp.mean(centered * centered, axis=-1, keepdims=True) + EPS)
    return (centered * inverse_std, inverse_std)


def normalize_back(grad_unit, unit_rows, inverse_std):
    plain_mean = jnp.mean(grad_unit, axis=-1, keepdims=True)
    cross_mean = jnp.mean(grad_unit * unit_rows, axis=-1, keepdims=True)
    return inverse_std * (grad_unit - plain_mean - unit_rows * cross_mean)


def plain(left_side, right_side):
    return jnp.dot(left_side, right_side, preferred_element_type=jnp.float32)


def contract_last(left_side, right_side):
    return lax.dot_general(
        left_side, right_side, (((1,), (1,)), ((), ())), preferred_element_type=jnp.float32
    )


def contract_first(left_side, right_side):
    return lax.dot_general(
        left_side, right_side, (((0,), (0,)), ((), ())), preferred_element_type=jnp.float32
    )


def gelu_slope(values):
    return 0.5 * (1.0 + lax.erf(values / math.sqrt(2.0))) + values * jnp.exp(
        -0.5 * values * values
    ) / math.sqrt(2.0 * math.pi)


def position():
    dp, core = lax.axis_index("dp"), lax.axis_index("tensor")
    zh, zl = lax.rem(lax.div(dp, 8), 2), lax.rem(lax.div(dp, 4), 2)
    y, x = lax.rem(lax.div(dp, 2), 2), lax.rem(dp, 2)
    peers = dict(
        core=(dp, 1 - core),
        x=(dp + 1 - 2 * x, core),
        y=(dp + 2 - 4 * y, core),
        zl=(dp + 4 - 8 * zl, core),
        zh=(dp + 8 - 16 * zh, core),
    )
    return core, zh, zl, y, x, peers


def greet(peers):
    barrier = pltpu.get_barrier_semaphore()
    for peer in peers.values():
        pl.semaphore_signal(barrier, inc=1, device_id=peer, device_id_type=MESH)
    pl.semaphore_wait(barrier, len(peers))


class Chunk:
    def __init__(self, groups, landed=None, first=None):
        self.groups, self.landed, self.first, self.stage = groups, landed, first, 0

    def advance(self):
        stage = self.stage
        if stage > len(self.groups):
            return
        if stage > 0:
            for copy in self.groups[stage - 1]:
                copy.wait_recv()
            if self.landed is not None:
                self.landed(stage - 1)
        if stage == 1 and self.first is not None:
            self.first.wait()
        if stage < len(self.groups):
            for copy in self.groups[stage]:
                copy.start()
        self.stage = stage + 1

    def finish(self):
        while self.stage <= len(self.groups):
            self.advance()

    def wait_sent(self):
        for group in self.groups:
            for copy in group:
                copy.wait_send()


def remote_maker(send_sem, recv_sem, peers):
    def remote(k, slot, source, target, peer):
        return pltpu.make_async_remote_copy(
            src_ref=source,
            dst_ref=target,
            send_sem=send_sem.at[k, slot],
            recv_sem=recv_sem.at[k, slot],
            device_id=peers[peer],
            device_id_type=MESH,
        )

    return remote


def vector_chunk(remote, k, start, totals, arrived):
    order = ("zh", "zl", "y", "x", "core")
    sources = [start] + [totals.at[i] for i in range(4)]
    groups = [
        [remote(k, i, sources[i], arrived.at[i], peer)] for i, peer in enumerate(order)
    ]

    def landed(i):
        totals[i] = (start[...] if i == 0 else totals[i - 1]) + arrived[i]

    return Chunk(groups, landed)


def forward_kernel(
    gain_part, attend_w, mixing_w, expand_w, reduce_w, tokens, cosine, sine, seg_rows, seg_cols,
    gain_out, attend_full, mixing_full, expand_full, reduce_full,
    normed_out, unit_out, inverse_out, q_out, k_out, v_out, att_out, log_out, cols_out,
    other_tokens, totals, arrived, own_sem, send_sem, recv_sem, token_sem,
):
    core, zh, zl, y, x, peers = position()
    remote = remote_maker(send_sem, recv_sem, peers)
    every = slice(None)
    own_rows = tokens.shape[0]
    pieces = [(attend_w, attend_full, 0), (attend_w, attend_full, 1), (attend_w, attend_full, 2)]
    pieces += [(mixing_w, mixing_full, 0), (expand_w, expand_full, 0)]
    pieces += [(expand_w, expand_full, 1), (reduce_w, reduce_full, 0)]
    chunks = [vector_chunk(remote, 0, gain_part, totals, arrived)]
    for k, (shard, full, j) in enumerate(pieces, 1):
        local = pltpu.make_async_copy(
            shard.at[j], full.at[core, j, zh, zl, y, x], own_sem.at[k]
        )
        local.start()

        def same(slot, index, peer, k=k, full=full, j=j):
            block = full.at[(core, j) + index]
            return remote(k, slot, block, block, peer)

        groups = [
            [remote(k, 0, shard.at[j], full.at[core, j, zh, zl, y, x], "zh")],
            [same(1, (every, zl, y, x), "zl")],
            [same(2, (every, 0, y, x), "x"), same(3, (every, 1, y, x), "y")],
            [same(4, (every, 0, y), "y"), same(5, (every, 1, every, x), "x")],
            [same(6, (), "core")],
        ]
        chunks.append(Chunk(groups, first=local))
    token_copy = pltpu.make_async_remote_copy(
        src_ref=tokens,
        dst_ref=other_tokens,
        send_sem=token_sem.at[0],
        recv_sem=token_sem.at[1],
        device_id=peers["core"],
        device_id_type=MESH,
    )
    greet(peers)
    token_copy.start()

    def own_unit():
        unit, inverse = normalize(tokens[...].astype(jnp.float32))
        unit_out[:own_rows], inverse_out[:own_rows] = unit, inverse

    def other_unit():
        token_copy.wait_recv()
        unit, inverse = normalize(other_tokens[...].astype(jnp.float32))
        unit_out[own_rows:], inverse_out[own_rows:] = unit, inverse

    def norm():
        gain_out[...] = totals[4]
        normed_out[...] = (unit_out[...] * totals[4, 0:1]).astype(jnp.bfloat16)

    def heads(p):
        def run():
            side, lanes = p // 3, slice((p % 3) * LANES, (p % 3 + 1) * LANES)
            wq, wk, wv = (
                attend_full[side, j, :, :, :, :, :, lanes].reshape(-1, LANES) for j in range(3)
            )
            query, keys, value, mixed, logs = attend_step(
                normed_out[:own_rows], normed_out[...], wq, wk, wv, cosine[...], sine[...],
                seg_rows[...] == seg_cols[...],
            )
            q_out[p], k_out[p], v_out[p] = query, keys, value
            att_out[p], log_out[p] = mixed, logs
            cols_out[:, p * LANES : (p + 1) * LANES] = mixed

        return run

    lag = 2
    events = [(k + lag * s, chunk.advance) for k, chunk in enumerate(chunks) for s in range(6)]
    events += [(4.5, own_unit), (7.5, other_unit), (5 * lag + 0.5, norm)]
    begin = 3 + 5 * lag
    events += [(begin + 0.1 + 0.65 * p, heads(p)) for p in range(6)]
    for _, event in sorted(events, key=lambda e: e[0]):
        event()
    for chunk in chunks:
        chunk.wait_sent()
    token_copy.wait_send()


def forward(gain_part, shards, tokens, cosine, sine, seg_rows, seg_cols):
    own, width = tokens.shape
    length, pairs = 2 * own, width // LANES
    blocks = [
        jax.ShapeDtypeStruct((2, s.shape[0], 2, 2, 2, 2) + s.shape[1:], s.dtype) for s in shards
    ]
    local = [
        jax.ShapeDtypeStruct((length, width), jnp.bfloat16),
        jax.ShapeDtypeStruct((length, width), jnp.float32),
        jax.ShapeDtypeStruct((length, 1), jnp.float32),
        jax.ShapeDtypeStruct((pairs, own, LANES), jnp.bfloat16),
        jax.ShapeDtypeStruct((pairs, length, LANES), jnp.bfloat16),
        jax.ShapeDtypeStruct((pairs, length, LANES), jnp.bfloat16),
        jax.ShapeDtypeStruct((pairs, own, LANES), jnp.bfloat16),
        jax.ShapeDtypeStruct((pairs, own, LANES), jnp.float32),
        jax.ShapeDtypeStruct((own, width), jnp.bfloat16),
    ]
    whole = pl.BlockSpec(memory_space=VMEM)
    anywhere = pl.BlockSpec(memory_space=pl.ANY)
    out = pl.pallas_call(
        forward_kernel,
        out_shape=[jax.ShapeDtypeStruct(gain_part.shape, jnp.float32)] + blocks + local,
        in_specs=[whole] + [anywhere] * 4 + [whole] * 5,
        out_specs=[whole, whole] + [anywhere] * 3 + [whole] * 9,
        scratch_shapes=[
            VMEM(tokens.shape, tokens.dtype),
            VMEM((5,) + gain_part.shape, jnp.float32),
            VMEM((5,) + gain_part.shape, jnp.float32),
            pltpu.SemaphoreType.DMA((8,)),
            pltpu.SemaphoreType.DMA((8, 7)),
            pltpu.SemaphoreType.DMA((8, 7)),
            pltpu.SemaphoreType.DMA((2,)),
        ],
        compiler_params=pltpu.CompilerParams(
            collective_id=0, has_side_effects=True, vmem_limit_bytes=VMEM_LIMIT
        ),
    )(gain_part, *shards, tokens, cosine, sine, seg_rows, seg_cols)
    return out[0], out[1:5], out[5:]


def backward_kernel(
    expand_part, reduce_part, attend_full, mixing_full, normed, unit, inverse, gains, second,
    branch, grad_middle, cosine, sine, seg_rows, seg_cols, q_in, k_in, v_in, att_in, log_in,
    attend_out, expand_out, reduce_out, gain_out, input_out,
    *scratch,
):
    kinds = 3
    attend_part, normed_grad, vector, totals, arrived, rows, other_rows = scratch[:7]
    buffers = scratch[7 : 7 + 5 * kinds]
    sums, firsts, seconds, thirds, fourths = (
        buffers[i * kinds : (i + 1) * kinds] for i in range(5)
    )
    send_sem, recv_sem, row_sem = scratch[7 + 5 * kinds :]
    parts, outs = (attend_part, expand_part, reduce_part), (attend_out, expand_out, reduce_out)
    core, zh, zl, y, x, peers = position()
    remote = remote_maker(send_sem, recv_sem, peers)
    every = slice(None)
    own = branch.shape[0]

    def reduce_chunk(k, kind, j):
        part, total, out = parts[kind], sums[kind], outs[kind]
        one, two, three, four = firsts[kind], seconds[kind], thirds[kind], fourths[kind]
        here = total.at[j]
        groups = [
            [remote(k, 0, part.at[1 - core, j], here, "core")],
            [
                remote(k, 1, here.at[every, 0, every, 1 - x], one.at[j, 0], "x"),
                remote(k, 2, here.at[every, 1, 1 - y], one.at[j, 1], "y"),
            ],
            [
                remote(k, 3, here.at[every, 0, 1 - y, x], two.at[j, 0], "y"),
                remote(k, 4, here.at[every, 1, y, 1 - x], two.at[j, 1], "x"),
            ],
            [remote(k, 5, here.at[every, 1 - zl, y, x], three.at[j], "zl")],
            [remote(k, 6, here.at[1 - zh, zl, y, x], four.at[j], "zh")],
        ]

        def landed(stage):
            if stage == 0:

                @pl.loop(0, 16)
                def _(b):
                    at = (
                        j, lax.div(b, 8), lax.rem(lax.div(b, 4), 2), lax.rem(lax.div(b, 2), 2),
                        lax.rem(b, 2),
                    )
                    total[at] = total[at] + part[(core,) + at]

            elif stage == 1:

                @pl.loop(0, 4)
                def _(b):
                    hi, lo = lax.div(b, 2), lax.rem(b, 2)
                    total[j, hi, 0, lo, x] = total[j, hi, 0, lo, x] + one[j, 0, hi, lo]
                    total[j, hi, 1, y, lo] = total[j, hi, 1, y, lo] + one[j, 1, hi, lo]

            elif stage == 2:

                @pl.loop(0, 2)
                def _(hi):
                    total[j, hi, 0, y, x] = total[j, hi, 0, y, x] + two[j, 0, hi]
                    total[j, hi, 1, y, x] = total[j, hi, 1, y, x] + two[j, 1, hi]

            elif stage == 3:

                @pl.loop(0, 2)
                def _(hi):
                    total[j, hi, zl, y, x] = total[j, hi, zl, y, x] + three[j, hi]

            else:
                last = total[j, zh, zl, y, x].astype(jnp.float32)
                out[j] = last + four[j].astype(jnp.float32)

        return Chunk(groups, landed)

    reduce_one, expand_a, expand_b = (
        reduce_chunk(0, 2, 0), reduce_chunk(1, 1, 0), reduce_chunk(2, 1, 1),
    )
    attends = [reduce_chunk(3 + g, 0, g) for g in range(3)]
    gain_chunk = vector_chunk(remote, 6, vector, totals, arrived)
    row_copy = pltpu.make_async_remote_copy(
        src_ref=rows,
        dst_ref=other_rows,
        send_sem=row_sem.at[0],
        recv_sem=row_sem.at[1],
        device_id=peers["core"],
        device_id_type=MESH,
    )

    def heads(side, g, initial):
        p = side * 3 + g
        lanes = slice(g * LANES, (g + 1) * LANES)
        wq, wk, wv = (attend_full[side, j, :, lanes] for j in range(3))
        weights, update, first = attend_back_step(
            normed[:own], normed[...], branch[...], wq, wk, wv, mixing_full[side, 0, :, lanes],
            cosine[...], sine[...], seg_rows[...] == seg_cols[...],
            q_in[p], k_in[p], v_in[p], att_in[p], log_in[p],
        )
        for j, block in enumerate(weights):
            spot = slice(j * 48, (j + 1) * 48)
            attend_part[side, g, :, :, :, :, spot, :] = block.reshape(2, 2, 2, 2, 48, LANES)
        if initial:
            normed_grad[...] = update
        else:
            normed_grad[...] += update
        normed_grad[:own] += first

    greet(peers)
    for chunk in (reduce_one, expand_a, expand_b):
        chunk.advance()
    heads(1 - core, 0, True)
    attends[0].advance()
    reduce_one.advance()
    expand_a.advance()
    heads(core, 0, False)
    for chunk in (reduce_one, expand_a, expand_b):
        chunk.advance()
    heads(1 - core, 1, False)
    attends[1].advance()
    for chunk in (reduce_one, expand_a, expand_b, attends[0]):
        chunk.advance()
    heads(core, 1, False)
    for chunk in (reduce_one, expand_a, expand_b, attends[0]):
        chunk.advance()
    heads(1 - core, 2, False)
    attends[2].advance()
    for chunk in (reduce_one, expand_a, expand_b, attends[0], attends[1]):
        chunk.advance()
    heads(core, 2, False)
    for chunk in (attends[2], attends[1], attends[0], expand_a, expand_b):
        chunk.advance()
    first_local = jnp.sum(normed_grad[...] * unit[...], axis=0, keepdims=True)
    vector[...] = jnp.zeros_like(vector)
    vector[0:1] = first_local
    vector[1:2] = second[...]
    gain_chunk.advance()
    gain = gains[0:1]
    rows[...] = normalize_back(normed_grad[own:] * gain, unit[own:], inverse[own:]).astype(
        jnp.bfloat16
    )
    row_copy.start()
    for chunk in (attends[0], attends[1], attends[2], gain_chunk):
        chunk.advance()
    input_out[...] = grad_middle[...] + normalize_back(
        normed_grad[:own] * gain, unit[:own], inverse[:own]
    )
    every_chunk = [attends[0], attends[1], attends[2], gain_chunk, expand_a, expand_b, reduce_one]
    while any(chunk.stage <= 5 for chunk in every_chunk):
        for chunk in every_chunk:
            if chunk.stage <= 5:
                chunk.advance()
    gain_out[...] = totals[4]
    row_copy.wait_recv()
    input_out[...] += other_rows[...].astype(jnp.float32)
    for chunk in every_chunk:
        chunk.wait_sent()
    row_copy.wait_send()


def backward(grad_expand, grad_reduce, fulls, normed, unit, inverse, gains, second, branch,
             grad_middle, tables, saved):
    own, width = branch.shape

    def split(part):
        rows = part.shape[2] // 16
        return part.reshape(part.shape[:2] + (2, 2, 2, 2, rows, part.shape[3]))

    grad_expand, grad_reduce = split(grad_expand), split(grad_reduce)
    attend_shape = (2, 3, 2, 2, 2, 2, 4 * grad_expand.shape[-2], LANES)
    shapes = [attend_shape, grad_expand.shape, grad_reduce.shape]

    def buffers(dims):
        return [VMEM((s[1],) + dims + s[-2:], jnp.bfloat16) for s in shapes]

    whole = pl.BlockSpec(memory_space=VMEM)
    args = (grad_expand, grad_reduce, fulls[0], fulls[1], normed, unit, inverse, gains, second,
            branch, grad_middle, *tables, *saved)
    return pl.pallas_call(
        backward_kernel,
        out_shape=[jax.ShapeDtypeStruct((s[1],) + s[-2:], jnp.float32) for s in shapes]
        + [
            jax.ShapeDtypeStruct(gains.shape, jnp.float32),
            jax.ShapeDtypeStruct((own, width), jnp.float32),
        ],
        in_specs=[whole] * len(args),
        out_specs=[whole] * 5,
        scratch_shapes=[
            VMEM(attend_shape, jnp.bfloat16),
            VMEM(normed.shape, jnp.float32),
            VMEM(gains.shape, jnp.float32),
            VMEM((5,) + gains.shape, jnp.float32),
            VMEM((5,) + gains.shape, jnp.float32),
            VMEM((own, width), jnp.bfloat16),
            VMEM((own, width), jnp.bfloat16),
        ]
        + buffers((2, 2, 2, 2))
        + buffers((2, 2, 2))
        + buffers((2, 2))
        + buffers((2,))
        + buffers(())
        + [
            pltpu.SemaphoreType.DMA((7, 7)),
            pltpu.SemaphoreType.DMA((7, 7)),
            pltpu.SemaphoreType.DMA((2,)),
        ],
        compiler_params=pltpu.CompilerParams(
            collective_id=1, has_side_effects=True, vmem_limit_bytes=VMEM_LIMIT
        ),
    )(*args)


def half_turn(values):
    lane = lax.broadcasted_iota(jnp.int32, values.shape, 1)
    low = lax.rem(lane, HEAD_SIZE) < HEAD_SIZE // 2
    shift = HEAD_SIZE // 2
    return jnp.where(
        low, -pltpu.roll(values, LANES - shift, 1), pltpu.roll(values, shift, 1)
    )


def attend_step(normed_own, normed, wq, wk, wv, cos, sin, allowed):
    own = normed_own.shape[0]
    query = plain(normed_own, wq)
    query = query * cos[:own] + half_turn(query) * sin[:own]
    query = (query * HEAD_SIZE**-0.5).astype(jnp.bfloat16)
    keys = plain(normed, wk)
    keys = (keys * cos + half_turn(keys) * sin).astype(jnp.bfloat16)
    value = plain(normed, wv).astype(jnp.bfloat16)
    mixed, logs = [], []
    for head in range(LANES // HEAD_SIZE):
        part = slice(head * HEAD_SIZE, (head + 1) * HEAD_SIZE)
        scores = jnp.where(allowed, contract_last(query[:, part], keys[:, part]), MASKED)
        peak = jnp.max(scores, axis=-1, keepdims=True)
        exponent = jnp.exp(scores - peak)
        total = jnp.sum(exponent, axis=-1, keepdims=True)
        probs = (exponent / total).astype(jnp.bfloat16)
        mixed.append(plain(probs, value[:, part]).astype(jnp.bfloat16))
        logs.append(jnp.broadcast_to(peak + jnp.log(total), (own, HEAD_SIZE)))
    return query, keys, value, jnp.concatenate(mixed, axis=1), jnp.concatenate(logs, axis=1)


def attend_back_step(
    normed_own, normed, branch, wq, wk, wv, mix, cos, sin, allowed, query, keys, value, attended,
    logs,
):
    own = normed_own.shape[0]
    grad = plain(branch, mix).astype(jnp.bfloat16)
    grad_q, grad_k, grad_v = [], [], []
    for head in range(LANES // HEAD_SIZE):
        part = slice(head * HEAD_SIZE, (head + 1) * HEAD_SIZE)
        qh, kh, vh, gh = query[:, part], keys[:, part], value[:, part], grad[:, part]
        scores = jnp.where(allowed, contract_last(qh, kh), MASKED)
        probs = jnp.exp(scores - logs[:, head * HEAD_SIZE : head * HEAD_SIZE + 1])
        grad_v.append(contract_first(probs.astype(jnp.bfloat16), gh))
        grad_probs = contract_last(gh, vh)
        inner = jnp.sum(grad_probs * probs, axis=-1, keepdims=True)
        grad_scores = (probs * (grad_probs - inner)).astype(jnp.bfloat16)
        grad_q.append(plain(grad_scores, kh))
        grad_k.append(contract_first(grad_scores, qh))
    gq = jnp.concatenate(grad_q, axis=1) * HEAD_SIZE**-0.5
    gk = jnp.concatenate(grad_k, axis=1)
    gv = jnp.concatenate(grad_v, axis=1).astype(jnp.bfloat16)
    gq = (gq * cos[:own] - half_turn(gq * sin[:own])).astype(jnp.bfloat16)
    gk = (gk * cos - half_turn(gk * sin)).astype(jnp.bfloat16)
    weights = (
        contract_first(normed_own, gq).astype(jnp.bfloat16),
        contract_first(normed, gk).astype(jnp.bfloat16),
        contract_first(normed, gv).astype(jnp.bfloat16),
        contract_first(branch, attended).astype(jnp.bfloat16),
    )
    update = contract_last(gk, wk) + contract_last(gv, wv)
    return weights, update, contract_last(gq, wq)


def attend_kernel(
    normed, wq, wk, wv, cosine, sine, seg_rows, seg_cols, q_out, k_out, v_out, att_out, log_out
):
    own = seg_rows.shape[0]
    q_out[0], k_out[0], v_out[0], att_out[0], log_out[0] = attend_step(
        normed[:own], normed[...], wq[0, 0], wk[0, 0], wv[0, 0], cosine[...], sine[...],
        seg_rows[...] == seg_cols[...],
    )


def attend_back_kernel(
    normed, branch, wq, wk, wv, mix, cosine, sine, seg_rows, seg_cols, q_in, k_in, v_in, att_in,
    log_in, weight_out, mix_out, normed_out,
):
    own = seg_rows.shape[0]
    step = pl.program_id(0)
    weights, update, first = attend_back_step(
        normed[:own], normed[...], branch[...], wq[0, 0], wk[0, 0], wv[0, 0], mix[0, 0],
        cosine[...], sine[...], seg_rows[...] == seg_cols[...], q_in[0], k_in[0], v_in[0],
        att_in[0], log_in[0],
    )
    for j in range(3):
        weight_out[0, j] = weights[j]
    mix_out[0, 0] = weights[3]

    @pl.when(step == 0)
    def _():
        normed_out[...] = update

    @pl.when(step > 0)
    def _():
        normed_out[...] += update

    normed_out[:own] += first


def attention_specs(width, own, length, groups):
    def weight(j):
        return pl.BlockSpec((1, 1, width, LANES), lambda p: (p // groups, j, 0, p % groups))

    def columns(rows):
        return pl.BlockSpec((1, rows, LANES), lambda p: (p, 0, 0))

    def whole(*shape):
        return pl.BlockSpec(shape, lambda p: (0,) * len(shape))

    return weight, columns, whole


def attend(normed, weights, cosine, sine, seg_rows, seg_cols):
    length, width = normed.shape
    own = seg_rows.shape[0]
    groups = weights.shape[3] // LANES
    weight, columns, whole = attention_specs(width, own, length, groups)
    pairs = 2 * groups
    return pl.pallas_call(
        attend_kernel,
        grid=(2 * groups,),
        out_shape=[
            jax.ShapeDtypeStruct((pairs, own, LANES), jnp.bfloat16),
            jax.ShapeDtypeStruct((pairs, length, LANES), jnp.bfloat16),
            jax.ShapeDtypeStruct((pairs, length, LANES), jnp.bfloat16),
            jax.ShapeDtypeStruct((pairs, own, LANES), jnp.bfloat16),
            jax.ShapeDtypeStruct((pairs, own, LANES), jnp.float32),
        ],
        in_specs=[
            whole(length, width), weight(0), weight(1), weight(2), whole(length, LANES),
            whole(length, LANES), whole(own, 1), whole(1, length),
        ],
        out_specs=[columns(own), columns(length), columns(length), columns(own), columns(own)],
        compiler_params=pltpu.CompilerParams(vmem_limit_bytes=VMEM_LIMIT),
    )(normed, weights, weights, weights, cosine, sine, seg_rows, seg_cols)


def attend_back(normed, branch, weights, mixing, cosine, sine, seg_rows, seg_cols, saved):
    length, width = normed.shape
    own = seg_rows.shape[0]
    groups = weights.shape[3] // LANES
    weight, columns, whole = attention_specs(width, own, length, groups)
    return pl.pallas_call(
        attend_back_kernel,
        grid=(2 * groups,),
        out_shape=[
            jax.ShapeDtypeStruct((2, 3, width, groups * LANES), jnp.bfloat16),
            jax.ShapeDtypeStruct((2, 1, width, groups * LANES), jnp.bfloat16),
            jax.ShapeDtypeStruct((length, width), jnp.float32),
        ],
        in_specs=[
            whole(length, width), whole(own, width), weight(0), weight(1), weight(2), weight(0),
            whole(length, LANES), whole(length, LANES), whole(own, 1), whole(1, length),
            columns(own), columns(length), columns(length), columns(own), columns(own),
        ],
        out_specs=[
            pl.BlockSpec((1, 3, width, LANES), lambda p: (p // groups, 0, 0, p % groups)),
            weight(0),
            whole(length, width),
        ],
        compiler_params=pltpu.CompilerParams(vmem_limit_bytes=VMEM_LIMIT),
    )(normed, branch, weights, weights, weights, mixing, cosine, sine, seg_rows, seg_cols, *saved)


def rotary_tables(length, core):
    indices = jnp.arange(HEAD_SIZE // 2, dtype=jnp.float32)
    inverse_freq = THETA ** (-(2.0 / HEAD_SIZE) * indices)
    angles = jnp.arange(length, dtype=jnp.float32)[:, None] * inverse_freq[None, :]
    angles = jnp.tile(angles, (1, LANES // (HEAD_SIZE // 2)))
    return own_first(jnp.cos(angles), core), own_first(jnp.sin(angles), core)


def own_first(rows, core):
    return jnp.where(core == 0, rows, jnp.roll(rows, rows.shape[0] // 2, axis=0))


def per_device(
    doubling,
    inputs,
    segments,
    gain_first,
    gain_second,
    attend_weight,
    mixing_matrix,
    expand_matrix,
    reduce_matrix,
    cotangent,
):
    core = lax.axis_index("tensor")
    own, width = inputs.shape
    length = segments.shape[0]
    share = gain_first.shape[0]
    shards = [attend_weight, mixing_matrix[None], expand_matrix, reduce_matrix[None]]
    cosine, sine = rotary_tables(length, core)
    segments = own_first(segments, core)
    seg_rows, seg_cols = segments[:own, None], segments[None, :]
    tables = (cosine, sine, seg_rows, seg_cols)
    place = (2 * lax.axis_index("dp") + core) * share
    if doubling:
        gains = jnp.zeros((8, width), jnp.float32)
        pair = jnp.stack([gain_first, gain_second])
        gains = lax.dynamic_update_slice(gains, pair, (jnp.int32(0), place))
        gains, fulls, local = forward(gains, shards, inputs, *tables)
        normed_one, unit_one, inverse_one = local[:3]
        saved, attended = local[3:8], local[8]
        full_first, full_second = gains[0], gains[1]
        fulls = [
            full.reshape((2, s.shape[0], 16 * s.shape[1], s.shape[2]))
            for full, s in zip(fulls, shards)
        ]
        attend_full, mixing_full, expand_full, reduce_full = fulls
        rows_in = inputs.astype(jnp.float32)
    else:
        both = ("dp", "tensor")
        full_first = lax.all_gather(gain_first, both, axis=0, tiled=True)
        full_second = lax.all_gather(gain_second, both, axis=0, tiled=True)
        attend_full, mixing_full, expand_full, reduce_full = (
            lax.all_gather(lax.all_gather(s, "dp", axis=1, tiled=True), "tensor", axis=0)
            for s in shards
        )
        pair = lax.all_gather(inputs, "tensor", axis=0)
        other_inputs = jnp.where(core == 0, pair[1], pair[0])
        rows_all = jnp.concatenate([inputs, other_inputs]).astype(jnp.float32)
        rows_in = rows_all[:own]
        unit_one, inverse_one = normalize(rows_all)
        normed_one = (unit_one * full_first).astype(jnp.bfloat16)
        saved = attend(normed_one, attend_full, *tables)
        attended = jnp.transpose(saved[3], (1, 0, 2)).reshape(own, width)
    half = attended.shape[1] // 2
    middle = (
        rows_in
        + contract_last(attended[:, :half], mixing_full[0, 0])
        + contract_last(attended[:, half:], mixing_full[1, 0])
    )
    unit_two, inverse_two = normalize(middle)
    normed_two = (unit_two * full_second).astype(jnp.bfloat16)
    output = middle
    grad_normed_two = jnp.zeros_like(middle)
    grad_expand, grad_reduce = [], []
    for side in range(2):
        activated_in = plain(normed_two, expand_full[side, 0])
        gate_linear = plain(normed_two, expand_full[side, 1])
        gelu_value = jax.nn.gelu(activated_in, approximate=False)
        hidden = (gelu_value * gate_linear).astype(jnp.bfloat16)
        output = output + contract_last(hidden, reduce_full[side, 0])
        grad_hidden = plain(cotangent, reduce_full[side, 0])
        grad_reduce.append(contract_first(cotangent, hidden).astype(jnp.bfloat16))
        grad_activated = (grad_hidden * gate_linear * gelu_slope(activated_in)).astype(
            jnp.bfloat16
        )
        grad_gate = (grad_hidden * gelu_value).astype(jnp.bfloat16)
        grad_expand.append(contract_first(normed_two, grad_activated).astype(jnp.bfloat16))
        grad_expand.append(contract_first(normed_two, grad_gate).astype(jnp.bfloat16))
        grad_normed_two = (
            grad_normed_two
            + contract_last(grad_activated, expand_full[side, 0])
            + contract_last(grad_gate, expand_full[side, 1])
        )
    hidden_width = expand_full.shape[3]
    grad_expand = jnp.stack(grad_expand).reshape(2, 2, width, hidden_width)
    grad_reduce = jnp.stack(grad_reduce).reshape(2, 1, width, hidden_width)
    second_local = jnp.sum(grad_normed_two * unit_two, axis=0)
    grad_middle = cotangent.astype(jnp.float32) + normalize_back(
        grad_normed_two * full_second, unit_two, inverse_two
    )
    grad_branch = grad_middle.astype(jnp.bfloat16)
    if doubling:
        sent_groups, sent_expand, sent_reduce, gains, input_grad = backward(
            grad_expand, grad_reduce, fulls, normed_one, unit_one, inverse_one, gains,
            second_local[None], grad_branch, grad_middle, tables, saved,
        )
        sent_groups = sent_groups.reshape(3, 4, -1, LANES)
        sent_groups = jnp.transpose(sent_groups, (1, 2, 0, 3)).reshape(4, -1, 3 * LANES)
        sent_attend, sent_mixing, sent_reduce = sent_groups[:3], sent_groups[3], sent_reduce[0]
        mine = lax.dynamic_slice(gains, (jnp.int32(0), place), (2, share))
        first_grad, second_grad = mine[0], mine[1]
    else:
        grad_attend, grad_mixing, grad_normed_one = attend_back(
            normed_one, grad_branch, attend_full, mixing_full, *tables, saved
        )
        first_local = jnp.sum(grad_normed_one * unit_one, axis=0)
        through = normalize_back(grad_normed_one * full_first, unit_one, inverse_one)
        rows_other = through[own:].astype(jnp.bfloat16)

        def summed(part):
            part = part.astype(jnp.float32)
            part = lax.psum_scatter(part, "tensor", scatter_dimension=0, tiled=False)
            return lax.psum_scatter(part, "dp", scatter_dimension=1, tiled=True)

        sent_attend, sent_expand = summed(grad_attend), summed(grad_expand)
        sent_mixing, sent_reduce = summed(grad_mixing)[0], summed(grad_reduce)[0]
        first_grad, second_grad = (
            lax.psum_scatter(part, ("dp", "tensor"), scatter_dimension=0, tiled=True)
            for part in (first_local, second_local)
        )
        pair = lax.all_gather(rows_other, "tensor", axis=0)
        rows_back = jnp.where(core == 0, pair[1], pair[0])
        input_grad = grad_middle + through[:own] + rows_back.astype(jnp.float32)
    return (
        output.astype(jnp.bfloat16),
        input_grad,
        first_grad,
        second_grad,
        sent_attend,
        sent_mixing,
        sent_expand,
        sent_reduce,
    )


def solution(mesh):
    in_specs = (
        P(("dp", "tensor"), None),
        P("dp"),
        P(("dp", "tensor")),
        P(("dp", "tensor")),
        P(None, "dp", "tensor"),
        P("dp", "tensor"),
        P(None, "dp", "tensor"),
        P("dp", "tensor"),
        P(("dp", "tensor"), None),
    )
    out_specs = (
        P(("dp", "tensor"), None),
        P(("dp", "tensor"), None),
        P(("dp", "tensor")),
        P(("dp", "tensor")),
        P(None, "dp", "tensor"),
        P("dp", "tensor"),
        P(None, "dp", "tensor"),
        P("dp", "tensor"),
    )
    doubling = mesh.shape["dp"] == 16 and mesh.shape["tensor"] == 2
    return jax.shard_map(
        functools.partial(per_device, doubling),
        mesh=mesh,
        in_specs=in_specs,
        out_specs=out_specs,
        check_vma=False,
    )
```

```python
import functools
import math

import jax
import jax.numpy as jnp
import numpy as np
from jax import lax
from jax.experimental import pallas as pl
from jax.experimental.pallas import tpu as pltpu
from jax.sharding import PartitionSpec as P

HEAD_SIZE = 64
EPS = 1e-05
THETA = 160000.0
MASKED = -1e30
LANES = 128
VMEM_LIMIT = 60 * 1024 * 1024
MESH = pl.DeviceIdType.MESH
VMEM = pltpu.VMEM


def normalize(values):
    centered = values - jnp.mean(values, axis=-1, keepdims=True)
    inverse_std = lax.rsqrt(jnp.mean(centered * centered, axis=-1, keepdims=True) + EPS)
    return (centered * inverse_std, inverse_std)


def normalize_back(grad_unit, unit_rows, inverse_std):
    plain_mean = jnp.mean(grad_unit, axis=-1, keepdims=True)
    cross_mean = jnp.mean(grad_unit * unit_rows, axis=-1, keepdims=True)
    return inverse_std * (grad_unit - plain_mean - unit_rows * cross_mean)


def plain(left_side, right_side):
    return jnp.dot(left_side, right_side, preferred_element_type=jnp.float32)


def contract_last(left_side, right_side):
    return lax.dot_general(
        left_side, right_side, (((1,), (1,)), ((), ())), preferred_element_type=jnp.float32
    )


def contract_first(left_side, right_side):
    return lax.dot_general(
        left_side, right_side, (((0,), (0,)), ((), ())), preferred_element_type=jnp.float32
    )


def gelu_slope(values):
    return 0.5 * (1.0 + lax.erf(values / math.sqrt(2.0))) + values * jnp.exp(
        -0.5 * values * values
    ) / math.sqrt(2.0 * math.pi)


def position():
    dp, core = lax.axis_index("dp"), lax.axis_index("tensor")
    zh, zl = lax.rem(lax.div(dp, 8), 2), lax.rem(lax.div(dp, 4), 2)
    y, x = lax.rem(lax.div(dp, 2), 2), lax.rem(dp, 2)
    peers = dict(
        core=(dp, 1 - core),
        x=(dp + 1 - 2 * x, core),
        y=(dp + 2 - 4 * y, core),
        zl=(dp + 4 - 8 * zl, core),
        zh=(dp + 8 - 16 * zh, core),
    )
    return core, zh, zl, y, x, peers


def greet(peers):
    barrier = pltpu.get_barrier_semaphore()
    for peer in peers.values():
        pl.semaphore_signal(barrier, inc=1, device_id=peer, device_id_type=MESH)
    pl.semaphore_wait(barrier, len(peers))


class Chunk:
    def __init__(self, groups, landed=None, first=None):
        self.groups, self.landed, self.first, self.stage = groups, landed, first, 0

    def advance(self):
        stage = self.stage
        if stage > len(self.groups):
            return
        if stage > 0:
            for copy in self.groups[stage - 1]:
                copy.wait_recv()
            if self.landed is not None:
                self.landed(stage - 1)
        if stage == 1 and self.first is not None:
            self.first.wait()
        if stage < len(self.groups):
            for copy in self.groups[stage]:
                copy.start()
        self.stage = stage + 1

    def finish(self):
        while self.stage <= len(self.groups):
            self.advance()

    def wait_sent(self):
        for group in self.groups:
            for copy in group:
                copy.wait_send()


def remote_maker(send_sem, recv_sem, peers):
    def remote(k, slot, source, target, peer):
        return pltpu.make_async_remote_copy(
            src_ref=source,
            dst_ref=target,
            send_sem=send_sem.at[k, slot],
            recv_sem=recv_sem.at[k, slot],
            device_id=peers[peer],
            device_id_type=MESH,
        )

    return remote


def vector_chunk(remote, k, start, totals, arrived):
    order = ("zh", "zl", "y", "x", "core")
    sources = [start] + [totals.at[i] for i in range(4)]
    groups = [
        [remote(k, i, sources[i], arrived.at[i], peer)] for i, peer in enumerate(order)
    ]

    def landed(i):
        totals[i] = (start[...] if i == 0 else totals[i - 1]) + arrived[i]

    return Chunk(groups, landed)


LAG = 2


def gather_groups(remote, k, shard, full, j, route, at):
    core, zh, zl, y, x = at
    every = slice(None)

    def same(slot, index, peer):
        block = full.at[(core, j) + index]
        return remote(k, slot, block, block, peer)

    start = [remote(k, 0, shard.at[j], full.at[core, j, zh, zl, y, x], "zh")]
    if route == "plane":
        middle = [
            [same(1, (every, zl, y, x), "zl")],
            [same(2, (every, 0, y, x), "x"), same(3, (every, 1, y, x), "y")],
            [same(4, (every, 0, y), "y"), same(5, (every, 1, every, x), "x")],
        ]
    elif route == "x":
        middle = [
            [same(1, (every, zl, y, x), "x")],
            [same(2, (every, zl, y), "y")],
            [same(3, (every, zl), "zl")],
        ]
    else:
        middle = [
            [same(1, (every, zl, y, x), "y")],
            [same(2, (every, zl, every, x), "x")],
            [same(3, (every, zl), "zl")],
        ]
    return [start] + middle + [[same(6, (), "core")]]


def reduce_chunk(remote, k, j, route, at, part, store, total, one, two, three, four):
    core, zh, zl, y, x = at
    every = slice(None)
    here = total.at[j]
    start = [remote(k, 0, part.at[1 - core, j], here, "core")]
    last = [remote(k, 6, here.at[1 - zh, zl, y, x], four.at[j], "zh")]
    if route == "plane":
        middle = [
            [
                remote(k, 1, here.at[every, 0, every, 1 - x], one.at[j, 0], "x"),
                remote(k, 2, here.at[every, 1, 1 - y], one.at[j, 1], "y"),
            ],
            [
                remote(k, 3, here.at[every, 0, 1 - y, x], two.at[j, 0], "y"),
                remote(k, 4, here.at[every, 1, y, 1 - x], two.at[j, 1], "x"),
            ],
            [remote(k, 5, here.at[every, 1 - zl, y, x], three.at[j], "zl")],
        ]
    elif route == "x":
        middle = [
            [remote(k, 1, here.at[every, 1 - zl], one.at[j], "zl")],
            [remote(k, 3, here.at[every, zl, 1 - y], two.at[j], "y")],
            [remote(k, 5, here.at[every, zl, y, 1 - x], three.at[j], "x")],
        ]
    else:
        middle = [
            [remote(k, 1, here.at[every, 1 - zl], one.at[j], "zl")],
            [remote(k, 3, here.at[every, zl, every, 1 - x], two.at[j], "x")],
            [remote(k, 5, here.at[every, zl, 1 - y, x], three.at[j], "y")],
        ]

    def bits(b):
        return lax.div(b, 4), lax.rem(lax.div(b, 2), 2), lax.rem(b, 2)

    def plus(index, value):
        total[(j,) + index] = total[(j,) + index] + value

    def landed(stage):
        if stage == 0:

            @pl.loop(0, 16)
            def _(b):
                index = (lax.div(b, 8),) + bits(lax.rem(b, 8))
                plus(index, part[(core, j) + index])

        elif stage == 1:

            @pl.loop(0, 8)
            def _(b):
                p, q, r = bits(b)
                if route == "plane":
                    @pl.when(p == 0)
                    def _():
                        plus((q, 0, r, x), one[j, 0, q, r])

                    @pl.when(p == 1)
                    def _():
                        plus((q, 1, y, r), one[j, 1, q, r])

                else:
                    plus((p, zl, q, r), one[j, p, q, r])

        elif stage == 2:

            @pl.loop(0, 4)
            def _(b):
                _, p, q = bits(b)
                if route == "plane":
                    plus((q, p, y, x), two[j, p, q])
                elif route == "x":
                    plus((p, zl, y, q), two[j, p, q])
                else:
                    plus((p, zl, q, x), two[j, p, q])

        elif stage == 3:

            @pl.loop(0, 2)
            def _(hi):
                plus((hi, zl, y, x), three[j, hi])

        else:
            store(total[j, zh, zl, y, x].astype(jnp.float32) + four[j].astype(jnp.float32))

    return Chunk([start] + middle + [last], landed)


def layer_kernel(
    gain_part, attend_w, mixing_w, expand_w, reduce_w, tokens, cotangent, cosine, sine, seg_rows,
    seg_cols,
    output, input_out, gain_out, attend_out, mixing_out, expand_out, reduce_out,
    attend_full, mixing_full, expand_full, reduce_full, attend_part, expand_part, reduce_part,
    sum_a, sum_e, sum_r, one_a, one_e, one_r, two_a, two_e, two_r, three_a, three_e, three_r,
    four_a, four_e, four_r,
    other_tokens, rows, other_rows, totals, arrived, vector, grad_totals, grad_arrived,
    cos, sin, normed, unit, inverse, queries, keys, values, mixed, logs, middle, unit_two,
    normed_two, normed_two_grad, grad_middle, branch, normed_grad,
    own_sem, send_sem, recv_sem, back_send_sem, back_recv_sem, pair_sem,
):
    core, zh, zl, y, x, peers = position()
    at = (core, zh, zl, y, x)
    own, width = tokens.shape
    pairs = width // LANES
    side_pairs = pairs // 2
    remote = remote_maker(send_sem, recv_sem, peers)
    back = remote_maker(back_send_sem, back_recv_sem, peers)

    pieces = [
        (attend_w, attend_full, 0, "plane"), (attend_w, attend_full, 1, "plane"),
        (attend_w, attend_full, 2, "x"), (mixing_w, mixing_full, 0, "plane"),
        (expand_w, expand_full, 0, "x"), (expand_w, expand_full, 1, "y"),
        (reduce_w, reduce_full, 0, "plane"),
    ]
    chunks = [vector_chunk(remote, 0, gain_part, totals, arrived)]
    for k, (shard, full, j, route) in enumerate(pieces, 1):
        local = pltpu.make_async_copy(
            shard.at[j], full.at[core, j, zh, zl, y, x], own_sem.at[k]
        )
        local.start()
        chunks.append(Chunk(gather_groups(remote, k, shard, full, j, route, at), first=local))

    def pair_copy(i, source, target):
        return pltpu.make_async_remote_copy(
            src_ref=source,
            dst_ref=target,
            send_sem=pair_sem.at[2 * i],
            recv_sem=pair_sem.at[2 * i + 1],
            device_id=peers["core"],
            device_id_type=MESH,
        )

    token_copy = pair_copy(0, tokens, other_tokens)
    row_copy = pair_copy(1, rows, other_rows)
    greet(peers)
    token_copy.start()

    def own_unit():
        mine, others = pl.ds(core * own, own), pl.ds((1 - core) * own, own)
        cos[:own], sin[:own] = cosine[mine], sine[mine]
        cos[own:], sin[own:] = cosine[others], sine[others]
        unit[:own], inverse[:own] = normalize(tokens[...].astype(jnp.float32))

    def other_unit():
        token_copy.wait_recv()
        unit[own:], inverse[own:] = normalize(other_tokens[...].astype(jnp.float32))

    def norm():
        normed[...] = (unit[...] * totals[4, 0:1]).astype(jnp.bfloat16)

    def attend_weights(side, g):
        lanes = slice(g * LANES, (g + 1) * LANES)
        return (attend_full[side, j, :, :, :, :, :, lanes].reshape(-1, LANES) for j in range(3))

    def heads(p):
        def run():
            wq, wk, wv = attend_weights(p // side_pairs, p % side_pairs)
            queries[p], keys[p], values[p], mixed[p], logs[p] = attend_step(
                normed[:own], normed[...], wq, wk, wv, cos[...], sin[...],
                seg_rows[...] == seg_cols[...],
            )

        return run

    def mix():
        summed = tokens[...].astype(jnp.float32)
        for side in range(2):
            columns = [mixed[side * side_pairs + g] for g in range(side_pairs)]
            weight = mixing_full[side, 0].reshape(width, -1)
            summed = summed + contract_last(jnp.concatenate(columns, axis=1), weight)
        middle[...] = summed

    events = [(k + LAG * s, chunk.advance) for k, chunk in enumerate(chunks) for s in range(6)]
    events += [(4.5, own_unit), (7.5, other_unit), (5 * LAG + 0.5, norm)]
    begin = 3 + 5 * LAG
    events += [(begin + 0.1 + 0.65 * p, heads(p)) for p in range(pairs)] + [(begin + 3.6, mix)]
    for _, event in sorted(events, key=lambda e: e[0]):
        event()

    unit_rows, inverse_two = normalize(middle[...])
    unit_two[...] = unit_rows
    normed_two[...] = (unit_rows * totals[4, 1:2]).astype(jnp.bfloat16)

    def feed(side, initial):
        weight_a, weight_g = (expand_full[side, j].reshape(width, -1) for j in range(2))
        weight_r = reduce_full[side, 0].reshape(width, -1)
        activated_in = plain(normed_two[...], weight_a)
        gate_linear = plain(normed_two[...], weight_g)
        spread = 0.5 * (1.0 + lax.erf(activated_in * math.sqrt(0.5)))
        gelu_value = activated_in * spread
        slope = spread + activated_in * jnp.exp(-0.5 * activated_in * activated_in) * (
            1.0 / math.sqrt(2.0 * math.pi)
        )
        hidden = (gelu_value * gate_linear).astype(jnp.bfloat16)
        grad_hidden = plain(cotangent[...], weight_r)
        grad_activated = (grad_hidden * gate_linear * slope).astype(jnp.bfloat16)
        grad_gate = (grad_hidden * gelu_value).astype(jnp.bfloat16)

        def split(value):
            return value.astype(jnp.bfloat16).reshape((2, 2, 2, 2, -1) + value.shape[1:])

        reduce_part[side, 0] = split(contract_first(cotangent[...], hidden))
        expand_part[side, 0] = split(contract_first(normed_two[...], grad_activated))
        expand_part[side, 1] = split(contract_first(normed_two[...], grad_gate))
        middle[...] += contract_last(hidden, weight_r)
        back_rows = contract_last(grad_activated, weight_a) + contract_last(grad_gate, weight_g)
        if initial:
            normed_two_grad[...] = back_rows
        else:
            normed_two_grad[...] += back_rows

    def store_plain(out, j):
        def store(value):
            out[j] = value

        return store

    def store_heads(g):
        lanes, share = slice(g * LANES, (g + 1) * LANES), mixing_out.shape[1]

        def store(value):
            for j in range(3):
                attend_out[j, :, lanes] = value[j * share : (j + 1) * share]
            mixing_out[0, :, lanes] = value[3 * share :]

        return store

    reduce_back = reduce_chunk(
        back, 0, 0, "plane", at, reduce_part, store_plain(reduce_out, 0), sum_r, one_r, two_r,
        three_r, four_r,
    )
    expand_back = [
        reduce_chunk(
            back, 1 + j, j, "xy"[j], at, expand_part, store_plain(expand_out, j), sum_e, one_e,
            two_e, three_e, four_e,
        )
        for j in range(2)
    ]
    attend_back_chunks = [
        reduce_chunk(
            back, 3 + g, g, ("plane", "x", "plane")[g], at, attend_part, store_heads(g), sum_a,
            one_a, two_a, three_a, four_a,
        )
        for g in range(side_pairs)
    ]
    gain_back = vector_chunk(back, 6, vector, grad_totals, grad_arrived)
    feed_chunks = [reduce_back] + expand_back

    def advance(*some):
        for chunk in some:
            chunk.advance()

    feed(1 - core, True)
    advance(*feed_chunks)
    feed(core, False)
    advance(*feed_chunks)
    output[...] = middle[...].astype(output.dtype)
    grad_rows = normed_two_grad[...]
    second_local = jnp.sum(grad_rows * unit_two[...], axis=0, keepdims=True)
    grad_middle[...] = cotangent[...].astype(jnp.float32) + normalize_back(
        grad_rows * totals[4, 1:2], unit_two[...], inverse_two
    )
    branch[...] = grad_middle[...].astype(jnp.bfloat16)

    def heads_back(side, g, initial):
        p = side * side_pairs + g
        wq, wk, wv = attend_weights(side, g)
        lanes = slice(g * LANES, (g + 1) * LANES)
        weights, update, first = attend_back_step(
            normed[:own], normed[...], branch[...], wq, wk, wv,
            mixing_full[side, 0, :, :, :, :, :, lanes].reshape(-1, LANES),
            cos[...], sin[...], seg_rows[...] == seg_cols[...],
            queries[p], keys[p], values[p], mixed[p], logs[p],
        )
        share = mixing_out.shape[1]
        for j, block in enumerate(weights):
            spot = slice(j * share, (j + 1) * share)
            attend_part[side, g, :, :, :, :, spot, :] = block.reshape(2, 2, 2, 2, share, LANES)
        if initial:
            normed_grad[...] = update
        else:
            normed_grad[...] += update
        normed_grad[:own] += first

    a0, a1, a2 = attend_back_chunks
    heads_back(1 - core, 0, True)
    advance(a0, *feed_chunks)
    heads_back(core, 0, False)
    advance(*feed_chunks)
    heads_back(1 - core, 1, False)
    advance(a1, *feed_chunks, a0)
    heads_back(core, 1, False)
    advance(*feed_chunks, a0, a1)
    heads_back(1 - core, 2, False)
    advance(a2, a0, a1, *feed_chunks)
    heads_back(core, 2, False)
    advance(a2, a1, a0)
    vector[...] = jnp.zeros_like(vector)
    vector[0:1] = jnp.sum(normed_grad[...] * unit[...], axis=0, keepdims=True)
    vector[1:2] = second_local
    advance(gain_back)
    gain = totals[4, 0:1]
    rows[...] = normalize_back(normed_grad[own:] * gain, unit[own:], inverse[own:]).astype(
        jnp.bfloat16
    )
    row_copy.start()
    advance(a0, a1, a2, gain_back)
    input_out[...] = grad_middle[...] + normalize_back(
        normed_grad[:own] * gain, unit[:own], inverse[:own]
    )
    backs = [a0, a1, a2, gain_back] + feed_chunks
    for _ in range(6):
        advance(*backs)
    gain_out[...] = grad_totals[4]
    row_copy.wait_recv()
    input_out[...] += other_rows[...].astype(jnp.float32)
    for chunk in chunks + backs:
        chunk.wait_sent()
    token_copy.wait_send()
    row_copy.wait_send()


def layer(gain_part, shards, tokens, cotangent, cosine, sine, seg_rows, seg_cols):
    own, width = tokens.shape
    length, pairs = 2 * own, width // LANES
    full, low = jnp.float32, jnp.bfloat16
    fulls = [VMEM((2, s.shape[0], 2, 2, 2, 2) + s.shape[1:], low) for s in shards]
    share, hidden = shards[2].shape[1:]
    parts = [
        (pairs // 2, 4 * share, LANES), (2, share, hidden), (1, share, hidden),
    ]

    def buffers(dims):
        return [VMEM(p[:1] + dims + p[1:], low) for p in parts]

    def rows(count, columns, dtype):
        return VMEM((count, columns), dtype)

    def stack(count, dtype):
        return VMEM((pairs, count, LANES), dtype)

    vectors = VMEM((5,) + gain_part.shape, full)
    whole = pl.BlockSpec(memory_space=VMEM)
    anywhere = pl.BlockSpec(memory_space=pl.ANY)
    dma = pltpu.SemaphoreType.DMA
    return pl.pallas_call(
        layer_kernel,
        out_shape=[
            jax.ShapeDtypeStruct((own, width), low),
            jax.ShapeDtypeStruct((own, width), full),
            jax.ShapeDtypeStruct(gain_part.shape, full),
        ]
        + [jax.ShapeDtypeStruct(s.shape, full) for s in shards],
        in_specs=[whole] + [anywhere] * 4 + [whole] * 6,
        out_specs=[whole] * 7,
        scratch_shapes=fulls
        + [VMEM((2,) + p[:1] + (2, 2, 2, 2) + p[1:], low) for p in parts]
        + buffers((2, 2, 2, 2))
        + buffers((2, 2, 2))
        + buffers((2, 2))
        + buffers((2,))
        + buffers(())
        + [rows(own, width, low)] * 3
        + [vectors, vectors, VMEM(gain_part.shape, full), vectors, vectors]
        + [rows(length, LANES, full)] * 2
        + [rows(length, width, low), rows(length, width, full), rows(length, 1, full)]
        + [stack(own, low), stack(length, low), stack(length, low), stack(own, low)]
        + [stack(own, full), rows(own, width, full), rows(own, width, full)]
        + [rows(own, width, low), rows(own, width, full), rows(own, width, full)]
        + [rows(own, width, low), rows(length, width, full)]
        + [dma((8,)), dma((8, 7)), dma((8, 7)), dma((7, 7)), dma((7, 7)), dma((4,))],
        compiler_params=pltpu.CompilerParams(
            collective_id=0, has_side_effects=True, vmem_limit_bytes=VMEM_LIMIT
        ),
    )(gain_part, *shards, tokens, cotangent, cosine, sine, seg_rows, seg_cols)


def half_turn(values):
    lane = lax.broadcasted_iota(jnp.int32, values.shape, 1)
    low = lax.rem(lane, HEAD_SIZE) < HEAD_SIZE // 2
    shift = HEAD_SIZE // 2
    return jnp.where(
        low, -pltpu.roll(values, LANES - shift, 1), pltpu.roll(values, shift, 1)
    )


def attend_step(normed_own, normed, wq, wk, wv, cos, sin, allowed):
    own = normed_own.shape[0]
    query = plain(normed_own, wq)
    query = query * cos[:own] + half_turn(query) * sin[:own]
    query = (query * HEAD_SIZE**-0.5).astype(jnp.bfloat16)
    keys = plain(normed, wk)
    keys = (keys * cos + half_turn(keys) * sin).astype(jnp.bfloat16)
    value = plain(normed, wv).astype(jnp.bfloat16)
    mixed, logs = [], []
    for head in range(LANES // HEAD_SIZE):
        part = slice(head * HEAD_SIZE, (head + 1) * HEAD_SIZE)
        scores = jnp.where(allowed, contract_last(query[:, part], keys[:, part]), MASKED)
        peak = jnp.max(scores, axis=-1, keepdims=True)
        exponent = jnp.exp(scores - peak)
        total = jnp.sum(exponent, axis=-1, keepdims=True)
        probs = (exponent / total).astype(jnp.bfloat16)
        mixed.append(plain(probs, value[:, part]).astype(jnp.bfloat16))
        logs.append(jnp.broadcast_to(peak + jnp.log(total), (own, HEAD_SIZE)))
    return query, keys, value, jnp.concatenate(mixed, axis=1), jnp.concatenate(logs, axis=1)


def attend_back_step(
    normed_own, normed, branch, wq, wk, wv, mix, cos, sin, allowed, query, keys, value, attended,
    logs,
):
    own = normed_own.shape[0]
    grad = plain(branch, mix).astype(jnp.bfloat16)
    grad_q, grad_k, grad_v = [], [], []
    for head in range(LANES // HEAD_SIZE):
        part = slice(head * HEAD_SIZE, (head + 1) * HEAD_SIZE)
        qh, kh, vh, gh = query[:, part], keys[:, part], value[:, part], grad[:, part]
        scores = jnp.where(allowed, contract_last(qh, kh), MASKED)
        probs = jnp.exp(scores - logs[:, head * HEAD_SIZE : head * HEAD_SIZE + 1])
        grad_v.append(contract_first(probs.astype(jnp.bfloat16), gh))
        grad_probs = contract_last(gh, vh)
        inner = jnp.sum(grad_probs * probs, axis=-1, keepdims=True)
        grad_scores = (probs * (grad_probs - inner)).astype(jnp.bfloat16)
        grad_q.append(plain(grad_scores, kh))
        grad_k.append(contract_first(grad_scores, qh))
    gq = jnp.concatenate(grad_q, axis=1) * HEAD_SIZE**-0.5
    gk = jnp.concatenate(grad_k, axis=1)
    gv = jnp.concatenate(grad_v, axis=1).astype(jnp.bfloat16)
    gq = (gq * cos[:own] - half_turn(gq * sin[:own])).astype(jnp.bfloat16)
    gk = (gk * cos - half_turn(gk * sin)).astype(jnp.bfloat16)
    weights = (
        contract_first(normed_own, gq).astype(jnp.bfloat16),
        contract_first(normed, gk).astype(jnp.bfloat16),
        contract_first(normed, gv).astype(jnp.bfloat16),
        contract_first(branch, attended).astype(jnp.bfloat16),
    )
    update = contract_last(gk, wk) + contract_last(gv, wv)
    return weights, update, contract_last(gq, wq)


def attend_kernel(
    normed, wq, wk, wv, cosine, sine, seg_rows, seg_cols, q_out, k_out, v_out, att_out, log_out
):
    own = seg_rows.shape[0]
    q_out[0], k_out[0], v_out[0], att_out[0], log_out[0] = attend_step(
        normed[:own], normed[...], wq[0, 0], wk[0, 0], wv[0, 0], cosine[...], sine[...],
        seg_rows[...] == seg_cols[...],
    )


def attend_back_kernel(
    normed, branch, wq, wk, wv, mix, cosine, sine, seg_rows, seg_cols, q_in, k_in, v_in, att_in,
    log_in, weight_out, mix_out, normed_out,
):
    own = seg_rows.shape[0]
    step = pl.program_id(0)
    weights, update, first = attend_back_step(
        normed[:own], normed[...], branch[...], wq[0, 0], wk[0, 0], wv[0, 0], mix[0, 0],
        cosine[...], sine[...], seg_rows[...] == seg_cols[...], q_in[0], k_in[0], v_in[0],
        att_in[0], log_in[0],
    )
    for j in range(3):
        weight_out[0, j] = weights[j]
    mix_out[0, 0] = weights[3]

    @pl.when(step == 0)
    def _():
        normed_out[...] = update

    @pl.when(step > 0)
    def _():
        normed_out[...] += update

    normed_out[:own] += first


def attention_specs(width, own, length, groups):
    def weight(j):
        return pl.BlockSpec((1, 1, width, LANES), lambda p: (p // groups, j, 0, p % groups))

    def columns(rows):
        return pl.BlockSpec((1, rows, LANES), lambda p: (p, 0, 0))

    def whole(*shape):
        return pl.BlockSpec(shape, lambda p: (0,) * len(shape))

    return weight, columns, whole


def attend(normed, weights, cosine, sine, seg_rows, seg_cols):
    length, width = normed.shape
    own = seg_rows.shape[0]
    groups = weights.shape[3] // LANES
    weight, columns, whole = attention_specs(width, own, length, groups)
    pairs = 2 * groups
    return pl.pallas_call(
        attend_kernel,
        grid=(2 * groups,),
        out_shape=[
            jax.ShapeDtypeStruct((pairs, own, LANES), jnp.bfloat16),
            jax.ShapeDtypeStruct((pairs, length, LANES), jnp.bfloat16),
            jax.ShapeDtypeStruct((pairs, length, LANES), jnp.bfloat16),
            jax.ShapeDtypeStruct((pairs, own, LANES), jnp.bfloat16),
            jax.ShapeDtypeStruct((pairs, own, LANES), jnp.float32),
        ],
        in_specs=[
            whole(length, width), weight(0), weight(1), weight(2), whole(length, LANES),
            whole(length, LANES), whole(own, 1), whole(1, length),
        ],
        out_specs=[columns(own), columns(length), columns(length), columns(own), columns(own)],
        compiler_params=pltpu.CompilerParams(vmem_limit_bytes=VMEM_LIMIT),
    )(normed, weights, weights, weights, cosine, sine, seg_rows, seg_cols)


def attend_back(normed, branch, weights, mixing, cosine, sine, seg_rows, seg_cols, saved):
    length, width = normed.shape
    own = seg_rows.shape[0]
    groups = weights.shape[3] // LANES
    weight, columns, whole = attention_specs(width, own, length, groups)
    return pl.pallas_call(
        attend_back_kernel,
        grid=(2 * groups,),
        out_shape=[
            jax.ShapeDtypeStruct((2, 3, width, groups * LANES), jnp.bfloat16),
            jax.ShapeDtypeStruct((2, 1, width, groups * LANES), jnp.bfloat16),
            jax.ShapeDtypeStruct((length, width), jnp.float32),
        ],
        in_specs=[
            whole(length, width), whole(own, width), weight(0), weight(1), weight(2), weight(0),
            whole(length, LANES), whole(length, LANES), whole(own, 1), whole(1, length),
            columns(own), columns(length), columns(length), columns(own), columns(own),
        ],
        out_specs=[
            pl.BlockSpec((1, 3, width, LANES), lambda p: (p // groups, 0, 0, p % groups)),
            weight(0),
            whole(length, width),
        ],
        compiler_params=pltpu.CompilerParams(vmem_limit_bytes=VMEM_LIMIT),
    )(normed, branch, weights, weights, weights, mixing, cosine, sine, seg_rows, seg_cols, *saved)


def rotary_tables(length):
    indices = np.arange(HEAD_SIZE // 2, dtype=np.float32)
    inverse_freq = np.float32(THETA) ** (np.float32(-2.0 / HEAD_SIZE) * indices)
    angles = np.arange(length, dtype=np.float32)[:, None] * inverse_freq[None, :]
    angles = np.tile(angles, (1, LANES // (HEAD_SIZE // 2))).astype(np.float32)
    return jnp.asarray(np.cos(angles)), jnp.asarray(np.sin(angles))


def own_first(rows, core):
    return jnp.where(core == 0, rows, jnp.roll(rows, rows.shape[0] // 2, axis=0))


def per_device(
    doubling,
    inputs,
    segments,
    gain_first,
    gain_second,
    attend_weight,
    mixing_matrix,
    expand_matrix,
    reduce_matrix,
    cotangent,
):
    core = lax.axis_index("tensor")
    own, width = inputs.shape
    length = segments.shape[0]
    share = gain_first.shape[0]
    shards = [attend_weight, mixing_matrix[None], expand_matrix, reduce_matrix[None]]
    cosine, sine = rotary_tables(length)
    segments = own_first(segments, core)
    seg_rows, seg_cols = segments[:own, None], segments[None, :]
    place = (2 * lax.axis_index("dp") + core) * share
    if doubling:
        gains = jnp.zeros((8, width), jnp.float32)
        pair = jnp.stack([gain_first, gain_second])
        gains = lax.dynamic_update_slice(gains, pair, (jnp.int32(0), place))
        output, input_grad, gains, sent_attend, sent_mixing, sent_expand, sent_reduce = layer(
            gains, shards, inputs, cotangent, cosine, sine, seg_rows, seg_cols
        )
        mine = lax.dynamic_slice(gains, (jnp.int32(0), place), (2, share))
        return (
            output, input_grad, mine[0], mine[1], sent_attend, sent_mixing[0], sent_expand,
            sent_reduce[0],
        )
    tables = (own_first(cosine, core), own_first(sine, core), seg_rows, seg_cols)
    both = ("dp", "tensor")
    full_first = lax.all_gather(gain_first, both, axis=0, tiled=True)
    full_second = lax.all_gather(gain_second, both, axis=0, tiled=True)
    attend_full, mixing_full, expand_full, reduce_full = (
        lax.all_gather(lax.all_gather(s, "dp", axis=1, tiled=True), "tensor", axis=0)
        for s in shards
    )
    pair = lax.all_gather(inputs, "tensor", axis=0)
    other_inputs = jnp.where(core == 0, pair[1], pair[0])
    rows_all = jnp.concatenate([inputs, other_inputs]).astype(jnp.float32)
    rows_in = rows_all[:own]
    unit_one, inverse_one = normalize(rows_all)
    normed_one = (unit_one * full_first).astype(jnp.bfloat16)
    saved = attend(normed_one, attend_full, *tables)
    attended = jnp.transpose(saved[3], (1, 0, 2)).reshape(own, width)
    half = attended.shape[1] // 2
    middle = (
        rows_in
        + contract_last(attended[:, :half], mixing_full[0, 0])
        + contract_last(attended[:, half:], mixing_full[1, 0])
    )
    unit_two, inverse_two = normalize(middle)
    normed_two = (unit_two * full_second).astype(jnp.bfloat16)
    output = middle
    grad_normed_two = jnp.zeros_like(middle)
    grad_expand, grad_reduce = [], []
    for side in range(2):
        activated_in = plain(normed_two, expand_full[side, 0])
        gate_linear = plain(normed_two, expand_full[side, 1])
        gelu_value = jax.nn.gelu(activated_in, approximate=False)
        hidden = (gelu_value * gate_linear).astype(jnp.bfloat16)
        output = output + contract_last(hidden, reduce_full[side, 0])
        grad_hidden = plain(cotangent, reduce_full[side, 0])
        grad_reduce.append(contract_first(cotangent, hidden).astype(jnp.bfloat16))
        grad_activated = (grad_hidden * gate_linear * gelu_slope(activated_in)).astype(
            jnp.bfloat16
        )
        grad_gate = (grad_hidden * gelu_value).astype(jnp.bfloat16)
        grad_expand.append(contract_first(normed_two, grad_activated).astype(jnp.bfloat16))
        grad_expand.append(contract_first(normed_two, grad_gate).astype(jnp.bfloat16))
        grad_normed_two = (
            grad_normed_two
            + contract_last(grad_activated, expand_full[side, 0])
            + contract_last(grad_gate, expand_full[side, 1])
        )
    hidden_width = expand_full.shape[3]
    grad_expand = jnp.stack(grad_expand).reshape(2, 2, width, hidden_width)
    grad_reduce = jnp.stack(grad_reduce).reshape(2, 1, width, hidden_width)
    second_local = jnp.sum(grad_normed_two * unit_two, axis=0)
    grad_middle = cotangent.astype(jnp.float32) + normalize_back(
        grad_normed_two * full_second, unit_two, inverse_two
    )
    grad_branch = grad_middle.astype(jnp.bfloat16)
    grad_attend, grad_mixing, grad_normed_one = attend_back(
        normed_one, grad_branch, attend_full, mixing_full, *tables, saved
    )
    first_local = jnp.sum(grad_normed_one * unit_one, axis=0)
    through = normalize_back(grad_normed_one * full_first, unit_one, inverse_one)
    rows_other = through[own:].astype(jnp.bfloat16)

    def summed(part):
        part = part.astype(jnp.float32)
        part = lax.psum_scatter(part, "tensor", scatter_dimension=0, tiled=False)
        return lax.psum_scatter(part, "dp", scatter_dimension=1, tiled=True)

    sent_attend, sent_expand = summed(grad_attend), summed(grad_expand)
    sent_mixing, sent_reduce = summed(grad_mixing)[0], summed(grad_reduce)[0]
    first_grad, second_grad = (
        lax.psum_scatter(part, ("dp", "tensor"), scatter_dimension=0, tiled=True)
        for part in (first_local, second_local)
    )
    pair = lax.all_gather(rows_other, "tensor", axis=0)
    rows_back = jnp.where(core == 0, pair[1], pair[0])
    input_grad = grad_middle + through[:own] + rows_back.astype(jnp.float32)
    return (
        output.astype(jnp.bfloat16),
        input_grad,
        first_grad,
        second_grad,
        sent_attend,
        sent_mixing,
        sent_expand,
        sent_reduce,
    )


def solution(mesh):
    in_specs = (
        P(("dp", "tensor"), None),
        P("dp"),
        P(("dp", "tensor")),
        P(("dp", "tensor")),
        P(None, "dp", "tensor"),
        P("dp", "tensor"),
        P(None, "dp", "tensor"),
        P("dp", "tensor"),
        P(("dp", "tensor"), None),
    )
    out_specs = (
        P(("dp", "tensor"), None),
        P(("dp", "tensor"), None),
        P(("dp", "tensor")),
        P(("dp", "tensor")),
        P(None, "dp", "tensor"),
        P("dp", "tensor"),
        P(None, "dp", "tensor"),
        P("dp", "tensor"),
    )
    doubling = mesh.shape["dp"] == 16 and mesh.shape["tensor"] == 2
    return jax.shard_map(
        functools.partial(per_device, doubling),
        mesh=mesh,
        in_specs=in_specs,
        out_specs=out_specs,
        check_vma=False,
    )
```

```python
import functools
import math

import jax
import jax.numpy as jnp
import numpy as np
from jax import lax
from jax.experimental import pallas as pl
from jax.experimental.pallas import tpu as pltpu
from jax.sharding import PartitionSpec as P

HEAD_SIZE = 64
EPS = 1e-05
THETA = 160000.0
MASKED = -1e30
LANES = 128
VMEM_LIMIT = 60 * 1024 * 1024
MESH = pl.DeviceIdType.MESH
VMEM = pltpu.VMEM


def normalize(values):
    centered = values - jnp.mean(values, axis=-1, keepdims=True)
    inverse_std = lax.rsqrt(jnp.mean(centered * centered, axis=-1, keepdims=True) + EPS)
    return (centered * inverse_std, inverse_std)


def normalize_back(grad_unit, unit_rows, inverse_std):
    plain_mean = jnp.mean(grad_unit, axis=-1, keepdims=True)
    cross_mean = jnp.mean(grad_unit * unit_rows, axis=-1, keepdims=True)
    return inverse_std * (grad_unit - plain_mean - unit_rows * cross_mean)


def plain(left_side, right_side):
    return jnp.dot(left_side, right_side, preferred_element_type=jnp.float32)


def contract_last(left_side, right_side):
    return lax.dot_general(
        left_side, right_side, (((1,), (1,)), ((), ())), preferred_element_type=jnp.float32
    )


def contract_first(left_side, right_side):
    return lax.dot_general(
        left_side, right_side, (((0,), (0,)), ((), ())), preferred_element_type=jnp.float32
    )


def gelu_slope(values):
    return 0.5 * (1.0 + lax.erf(values / math.sqrt(2.0))) + values * jnp.exp(
        -0.5 * values * values
    ) / math.sqrt(2.0 * math.pi)


def position():
    dp, core = lax.axis_index("dp"), lax.axis_index("tensor")
    zh, zl = lax.rem(lax.div(dp, 8), 2), lax.rem(lax.div(dp, 4), 2)
    y, x = lax.rem(lax.div(dp, 2), 2), lax.rem(dp, 2)
    peers = dict(
        core=(dp, 1 - core),
        x=(dp + 1 - 2 * x, core),
        y=(dp + 2 - 4 * y, core),
        zl=(dp + 4 - 8 * zl, core),
        zh=(dp + 8 - 16 * zh, core),
    )
    return core, zh, zl, y, x, peers


def greet(peers):
    barrier = pltpu.get_barrier_semaphore()
    for peer in peers.values():
        pl.semaphore_signal(barrier, inc=1, device_id=peer, device_id_type=MESH)
    pl.semaphore_wait(barrier, len(peers))


class Chunk:
    def __init__(self, groups, landed=None, first=None):
        self.groups, self.landed, self.first, self.stage = groups, landed, first, 0

    def advance(self):
        stage = self.stage
        if stage > len(self.groups):
            return
        if stage > 0:
            for copy in self.groups[stage - 1]:
                copy.wait_recv()
            if self.landed is not None:
                self.landed(stage - 1)
        if stage == 1 and self.first is not None:
            self.first.wait()
        if stage < len(self.groups):
            for copy in self.groups[stage]:
                copy.start()
        self.stage = stage + 1

    def finish(self):
        while self.stage <= len(self.groups):
            self.advance()

    def wait_sent(self):
        for group in self.groups:
            for copy in group:
                copy.wait_send()


def remote_maker(send_sem, recv_sem, peers):
    def remote(k, slot, source, target, peer):
        return pltpu.make_async_remote_copy(
            src_ref=source,
            dst_ref=target,
            send_sem=send_sem.at[k, slot],
            recv_sem=recv_sem.at[k, slot],
            device_id=peers[peer],
            device_id_type=MESH,
        )

    return remote


def vector_chunk(remote, k, start, totals, arrived):
    order = ("zh", "zl", "y", "x", "core")
    sources = [start] + [totals.at[i] for i in range(4)]
    groups = [
        [remote(k, i, sources[i], arrived.at[i], peer)] for i, peer in enumerate(order)
    ]

    def landed(i):
        totals[i] = (start[...] if i == 0 else totals[i - 1]) + arrived[i]

    return Chunk(groups, landed)


def gather_groups(remote, k, shard, full, j, route, at):
    core, zh, zl, y, x = at
    every = slice(None)

    def same(slot, index, peer):
        block = full.at[(core, j) + index]
        return remote(k, slot, block, block, peer)

    start = [remote(k, 0, shard.at[j], full.at[core, j, zh, zl, y, x], "zh")]
    if route == "plane":
        middle = [
            [same(1, (every, zl, y, x), "zl")],
            [same(2, (every, 0, y, x), "x"), same(3, (every, 1, y, x), "y")],
            [same(4, (every, 0, y), "y"), same(5, (every, 1, every, x), "x")],
        ]
    elif route == "x":
        middle = [
            [same(1, (every, zl, y, x), "x")],
            [same(2, (every, zl, y), "y")],
            [same(3, (every, zl), "zl")],
        ]
    else:
        middle = [
            [same(1, (every, zl, y, x), "y")],
            [same(2, (every, zl, every, x), "x")],
            [same(3, (every, zl), "zl")],
        ]
    return [start] + middle + [[same(6, (), "core")]]


def reduce_chunk(remote, k, j, route, at, part, store, total, one, two, three, four):
    core, zh, zl, y, x = at
    every = slice(None)
    here = total.at[j]
    start = [remote(k, 0, part.at[1 - core, j], here, "core")]
    last = [remote(k, 6, here.at[1 - zh, zl, y, x], four.at[j], "zh")]
    if route == "plane":
        middle = [
            [
                remote(k, 1, here.at[every, 0, every, 1 - x], one.at[j, 0], "x"),
                remote(k, 2, here.at[every, 1, 1 - y], one.at[j, 1], "y"),
            ],
            [
                remote(k, 3, here.at[every, 0, 1 - y, x], two.at[j, 0], "y"),
                remote(k, 4, here.at[every, 1, y, 1 - x], two.at[j, 1], "x"),
            ],
            [remote(k, 5, here.at[every, 1 - zl, y, x], three.at[j], "zl")],
        ]
    elif route == "x":
        middle = [
            [remote(k, 1, here.at[every, 1 - zl], one.at[j], "zl")],
            [remote(k, 3, here.at[every, zl, 1 - y], two.at[j], "y")],
            [remote(k, 5, here.at[every, zl, y, 1 - x], three.at[j], "x")],
        ]
    else:
        middle = [
            [remote(k, 1, here.at[every, 1 - zl], one.at[j], "zl")],
            [remote(k, 3, here.at[every, zl, every, 1 - x], two.at[j], "x")],
            [remote(k, 5, here.at[every, zl, 1 - y, x], three.at[j], "y")],
        ]

    def bits(b):
        return lax.div(b, 4), lax.rem(lax.div(b, 2), 2), lax.rem(b, 2)

    def plus(index, value):
        total[(j,) + index] = total[(j,) + index] + value

    def landed(stage):
        if stage == 0:

            @pl.loop(0, 16)
            def _(b):
                index = (lax.div(b, 8),) + bits(lax.rem(b, 8))
                plus(index, part[(core, j) + index])

        elif stage == 1:

            @pl.loop(0, 8)
            def _(b):
                p, q, r = bits(b)
                if route == "plane":
                    @pl.when(p == 0)
                    def _():
                        plus((q, 0, r, x), one[j, 0, q, r])

                    @pl.when(p == 1)
                    def _():
                        plus((q, 1, y, r), one[j, 1, q, r])

                else:
                    plus((p, zl, q, r), one[j, p, q, r])

        elif stage == 2:

            @pl.loop(0, 4)
            def _(b):
                _, p, q = bits(b)
                if route == "plane":
                    plus((q, p, y, x), two[j, p, q])
                elif route == "x":
                    plus((p, zl, y, q), two[j, p, q])
                else:
                    plus((p, zl, q, x), two[j, p, q])

        elif stage == 3:

            @pl.loop(0, 2)
            def _(hi):
                plus((hi, zl, y, x), three[j, hi])

        else:
            store(total[j, zh, zl, y, x].astype(jnp.float32) + four[j].astype(jnp.float32))

    return Chunk([start] + middle + [last], landed)


def layer_kernel(
    gain_part, attend_w, mixing_w, expand_w, reduce_w, tokens, cotangent, cosine, sine, seg_rows,
    seg_cols,
    output, input_out, gain_out, attend_out, mixing_out, expand_out, reduce_out,
    attend_full, mixing_full, expand_full, reduce_full, attend_part, expand_part, reduce_part,
    sum_a, sum_e, sum_r, one_a, one_e, one_r, two_a, two_e, two_r, three_a, three_e, three_r,
    four_a, four_e, four_r,
    other_tokens, rows, other_rows, totals, arrived, vector, grad_totals, grad_arrived,
    cos, sin, normed, unit, inverse, queries, keys, values, mixed, logs, middle, unit_two,
    normed_two, normed_two_grad, grad_middle, branch, normed_grad,
    own_sem, send_sem, recv_sem, back_send_sem, back_recv_sem, pair_sem,
):
    core, zh, zl, y, x, peers = position()
    at = (core, zh, zl, y, x)
    own, width = tokens.shape
    pairs = width // LANES
    side_pairs = pairs // 2
    remote = remote_maker(send_sem, recv_sem, peers)
    back = remote_maker(back_send_sem, back_recv_sem, peers)

    pieces = [
        (attend_w, attend_full, 0, "plane"), (attend_w, attend_full, 1, "plane"),
        (attend_w, attend_full, 2, "x"), (mixing_w, mixing_full, 0, "plane"),
        (expand_w, expand_full, 0, "x"), (expand_w, expand_full, 1, "y"),
        (reduce_w, reduce_full, 0, "plane"),
    ]
    chunks = [vector_chunk(remote, 0, gain_part, totals, arrived)]
    for k, (shard, full, j, route) in enumerate(pieces, 1):
        local = pltpu.make_async_copy(
            shard.at[j], full.at[core, j, zh, zl, y, x], own_sem.at[k]
        )
        local.start()
        chunks.append(Chunk(gather_groups(remote, k, shard, full, j, route, at), first=local))

    def pair_copy(i, source, target):
        return pltpu.make_async_remote_copy(
            src_ref=source,
            dst_ref=target,
            send_sem=pair_sem.at[2 * i],
            recv_sem=pair_sem.at[2 * i + 1],
            device_id=peers["core"],
            device_id_type=MESH,
        )

    token_copy = pair_copy(0, tokens, other_tokens)
    row_copy = pair_copy(1, rows, other_rows)
    greet(peers)
    token_copy.start()

    def own_unit():
        mine, others = pl.ds(core * own, own), pl.ds((1 - core) * own, own)
        cos[:own], sin[:own] = cosine[mine], sine[mine]
        cos[own:], sin[own:] = cosine[others], sine[others]
        unit[:own], inverse[:own] = normalize(tokens[...].astype(jnp.float32))

    def other_unit():
        token_copy.wait_recv()
        unit[own:], inverse[own:] = normalize(other_tokens[...].astype(jnp.float32))

    def norm():
        normed[...] = (unit[...] * totals[4, 0:1]).astype(jnp.bfloat16)

    def attend_weights(side, g):
        lanes = slice(g * LANES, (g + 1) * LANES)
        return (attend_full[side, j, :, :, :, :, :, lanes].reshape(-1, LANES) for j in range(3))

    def heads(p):
        def run():
            wq, wk, wv = attend_weights(p // side_pairs, p % side_pairs)
            queries[p], keys[p], values[p], mixed[p], logs[p] = attend_step(
                normed[:own], normed[...], wq, wk, wv, cos[...], sin[...],
                seg_rows[...] == seg_cols[...],
            )

        return run

    def mix():
        summed = tokens[...].astype(jnp.float32)
        for side in range(2):
            columns = [mixed[side * side_pairs + g] for g in range(side_pairs)]
            weight = mixing_full[side, 0].reshape(width, -1)
            summed = summed + contract_last(jnp.concatenate(columns, axis=1), weight)
        middle[...] = summed

    offsets = (0, 1, 2, 3) + tuple(11.5 + 2 * i for i in range(4))
    events = [
        (offset + 4 * s, chunk.advance) for offset, chunk in zip(offsets, chunks) for s in range(6)
    ]
    events += [(5.5, own_unit), (9.5, other_unit), (20.5, norm)]
    events += [(23.1 + 1.6 * p, heads(p)) for p in range(pairs)] + [(23.2 + 1.6 * pairs, mix)]
    for _, event in sorted(events, key=lambda e: e[0]):
        event()

    unit_rows, inverse_two = normalize(middle[...])
    unit_two[...] = unit_rows
    normed_two[...] = (unit_rows * totals[4, 1:2]).astype(jnp.bfloat16)

    def feed(side, initial):
        weight_a, weight_g = (expand_full[side, j].reshape(width, -1) for j in range(2))
        weight_r = reduce_full[side, 0].reshape(width, -1)
        activated_in = plain(normed_two[...], weight_a)
        gate_linear = plain(normed_two[...], weight_g)
        spread = 0.5 * (1.0 + lax.erf(activated_in * math.sqrt(0.5)))
        gelu_value = activated_in * spread
        slope = spread + activated_in * jnp.exp(-0.5 * activated_in * activated_in) * (
            1.0 / math.sqrt(2.0 * math.pi)
        )
        hidden = (gelu_value * gate_linear).astype(jnp.bfloat16)
        grad_hidden = plain(cotangent[...], weight_r)
        grad_activated = (grad_hidden * gate_linear * slope).astype(jnp.bfloat16)
        grad_gate = (grad_hidden * gelu_value).astype(jnp.bfloat16)

        def split(value):
            return value.astype(jnp.bfloat16).reshape((2, 2, 2, 2, -1) + value.shape[1:])

        reduce_part[side, 0] = split(contract_first(cotangent[...], hidden))
        expand_part[side, 0] = split(contract_first(normed_two[...], grad_activated))
        expand_part[side, 1] = split(contract_first(normed_two[...], grad_gate))
        middle[...] += contract_last(hidden, weight_r)
        back_rows = contract_last(grad_activated, weight_a) + contract_last(grad_gate, weight_g)
        if initial:
            normed_two_grad[...] = back_rows
        else:
            normed_two_grad[...] += back_rows

    def store_plain(out, j):
        def store(value):
            out[j] = value

        return store

    def store_heads(g):
        lanes, share = slice(g * LANES, (g + 1) * LANES), mixing_out.shape[1]

        def store(value):
            for j in range(3):
                attend_out[j, :, lanes] = value[j * share : (j + 1) * share]
            mixing_out[0, :, lanes] = value[3 * share :]

        return store

    reduce_back = reduce_chunk(
        back, 0, 0, "plane", at, reduce_part, store_plain(reduce_out, 0), sum_r, one_r, two_r,
        three_r, four_r,
    )
    expand_back = [
        reduce_chunk(
            back, 1 + j, j, "xy"[j], at, expand_part, store_plain(expand_out, j), sum_e, one_e,
            two_e, three_e, four_e,
        )
        for j in range(2)
    ]
    attend_back_chunks = [
        reduce_chunk(
            back, 3 + g, g, ("plane", "x", "plane")[g], at, attend_part, store_heads(g), sum_a,
            one_a, two_a, three_a, four_a,
        )
        for g in range(side_pairs)
    ]
    gain_back = vector_chunk(back, 6, vector, grad_totals, grad_arrived)
    feed_chunks = [reduce_back] + expand_back

    def advance(*some):
        for chunk in some:
            chunk.advance()

    feed(1 - core, True)
    advance(*feed_chunks)
    feed(core, False)
    advance(*feed_chunks)
    output[...] = middle[...].astype(output.dtype)
    grad_rows = normed_two_grad[...]
    second_local = jnp.sum(grad_rows * unit_two[...], axis=0, keepdims=True)
    grad_middle[...] = cotangent[...].astype(jnp.float32) + normalize_back(
        grad_rows * totals[4, 1:2], unit_two[...], inverse_two
    )
    branch[...] = grad_middle[...].astype(jnp.bfloat16)

    def heads_back(side, g, initial):
        p = side * side_pairs + g
        wq, wk, wv = attend_weights(side, g)
        lanes = slice(g * LANES, (g + 1) * LANES)
        weights, update, first = attend_back_step(
            normed[:own], normed[...], branch[...], wq, wk, wv,
            mixing_full[side, 0, :, :, :, :, :, lanes].reshape(-1, LANES),
            cos[...], sin[...], seg_rows[...] == seg_cols[...],
            queries[p], keys[p], values[p], mixed[p], logs[p],
        )
        share = mixing_out.shape[1]
        for j, block in enumerate(weights):
            spot = slice(j * share, (j + 1) * share)
            attend_part[side, g, :, :, :, :, spot, :] = block.reshape(2, 2, 2, 2, share, LANES)
        if initial:
            normed_grad[...] = update
        else:
            normed_grad[...] += update
        normed_grad[:own] += first

    a0, a1, a2 = attend_back_chunks
    heads_back(1 - core, 0, True)
    advance(a0, *feed_chunks)
    heads_back(core, 0, False)
    advance(*feed_chunks)
    heads_back(1 - core, 1, False)
    advance(a1, *feed_chunks, a0)
    heads_back(core, 1, False)
    advance(*feed_chunks, a0, a1)
    heads_back(1 - core, 2, False)
    advance(a2, a0, a1, *feed_chunks)
    heads_back(core, 2, False)
    advance(a2, a1, a0)
    vector[...] = jnp.zeros_like(vector)
    vector[0:1] = jnp.sum(normed_grad[...] * unit[...], axis=0, keepdims=True)
    vector[1:2] = second_local
    advance(gain_back)
    gain = totals[4, 0:1]
    rows[...] = normalize_back(normed_grad[own:] * gain, unit[own:], inverse[own:]).astype(
        jnp.bfloat16
    )
    row_copy.start()
    advance(a0, a1, a2, gain_back)
    input_out[...] = grad_middle[...] + normalize_back(
        normed_grad[:own] * gain, unit[:own], inverse[:own]
    )
    backs = [a0, a1, a2, gain_back] + feed_chunks
    for _ in range(6):
        advance(*backs)
    gain_out[...] = grad_totals[4]
    row_copy.wait_recv()
    input_out[...] += other_rows[...].astype(jnp.float32)
    for chunk in chunks + backs:
        chunk.wait_sent()
    token_copy.wait_send()
    row_copy.wait_send()


def layer(gain_part, shards, tokens, cotangent, cosine, sine, seg_rows, seg_cols):
    own, width = tokens.shape
    length, pairs = 2 * own, width // LANES
    full, low = jnp.float32, jnp.bfloat16
    fulls = [VMEM((2, s.shape[0], 2, 2, 2, 2) + s.shape[1:], low) for s in shards]
    share, hidden = shards[2].shape[1:]
    parts = [
        (pairs // 2, 4 * share, LANES), (2, share, hidden), (1, share, hidden),
    ]

    def buffers(dims):
        return [VMEM(p[:1] + dims + p[1:], low) for p in parts]

    def rows(count, columns, dtype):
        return VMEM((count, columns), dtype)

    def stack(count, dtype):
        return VMEM((pairs, count, LANES), dtype)

    vectors = VMEM((5,) + gain_part.shape, full)
    whole = pl.BlockSpec(memory_space=VMEM)
    anywhere = pl.BlockSpec(memory_space=pl.ANY)
    dma = pltpu.SemaphoreType.DMA
    return pl.pallas_call(
        layer_kernel,
        out_shape=[
            jax.ShapeDtypeStruct((own, width), low),
            jax.ShapeDtypeStruct((own, width), full),
            jax.ShapeDtypeStruct(gain_part.shape, full),
        ]
        + [jax.ShapeDtypeStruct(s.shape, full) for s in shards],
        in_specs=[whole] + [anywhere] * 4 + [whole] * 6,
        out_specs=[whole] * 7,
        scratch_shapes=fulls
        + [VMEM((2,) + p[:1] + (2, 2, 2, 2) + p[1:], low) for p in parts]
        + buffers((2, 2, 2, 2))
        + buffers((2, 2, 2))
        + buffers((2, 2))
        + buffers((2,))
        + buffers(())
        + [rows(own, width, low)] * 3
        + [vectors, vectors, VMEM(gain_part.shape, full), vectors, vectors]
        + [rows(length, LANES, full)] * 2
        + [rows(length, width, low), rows(length, width, full), rows(length, 1, full)]
        + [stack(own, low), stack(length, low), stack(length, low), stack(own, low)]
        + [stack(own, full), rows(own, width, full), rows(own, width, full)]
        + [rows(own, width, low), rows(own, width, full), rows(own, width, full)]
        + [rows(own, width, low), rows(length, width, full)]
        + [dma((8,)), dma((8, 7)), dma((8, 7)), dma((7, 7)), dma((7, 7)), dma((4,))],
        compiler_params=pltpu.CompilerParams(
            collective_id=0, has_side_effects=True, vmem_limit_bytes=VMEM_LIMIT
        ),
    )(gain_part, *shards, tokens, cotangent, cosine, sine, seg_rows, seg_cols)


def half_turn(values):
    lane = lax.broadcasted_iota(jnp.int32, values.shape, 1)
    low = lax.rem(lane, HEAD_SIZE) < HEAD_SIZE // 2
    shift = HEAD_SIZE // 2
    return jnp.where(
        low, -pltpu.roll(values, LANES - shift, 1), pltpu.roll(values, shift, 1)
    )


def attend_step(normed_own, normed, wq, wk, wv, cos, sin, allowed):
    own = normed_own.shape[0]
    query = plain(normed_own, wq)
    query = query * cos[:own] + half_turn(query) * sin[:own]
    query = (query * HEAD_SIZE**-0.5).astype(jnp.bfloat16)
    keys = plain(normed, wk)
    keys = (keys * cos + half_turn(keys) * sin).astype(jnp.bfloat16)
    value = plain(normed, wv).astype(jnp.bfloat16)
    mixed, logs = [], []
    for head in range(LANES // HEAD_SIZE):
        part = slice(head * HEAD_SIZE, (head + 1) * HEAD_SIZE)
        scores = jnp.where(allowed, contract_last(query[:, part], keys[:, part]), MASKED)
        peak = jnp.max(scores, axis=-1, keepdims=True)
        exponent = jnp.exp(scores - peak)
        total = jnp.sum(exponent, axis=-1, keepdims=True)
        probs = (exponent * (1.0 / total)).astype(jnp.bfloat16)
        mixed.append(plain(probs, value[:, part]).astype(jnp.bfloat16))
        logs.append(jnp.broadcast_to(peak + jnp.log(total), (own, HEAD_SIZE)))
    return query, keys, value, jnp.concatenate(mixed, axis=1), jnp.concatenate(logs, axis=1)


def attend_back_step(
    normed_own, normed, branch, wq, wk, wv, mix, cos, sin, allowed, query, keys, value, attended,
    logs,
):
    own = normed_own.shape[0]
    grad = plain(branch, mix).astype(jnp.bfloat16)
    grad_q, grad_k, grad_v = [], [], []
    for head in range(LANES // HEAD_SIZE):
        part = slice(head * HEAD_SIZE, (head + 1) * HEAD_SIZE)
        qh, kh, vh, gh = query[:, part], keys[:, part], value[:, part], grad[:, part]
        scores = jnp.where(allowed, contract_last(qh, kh), MASKED)
        probs = jnp.exp(scores - logs[:, head * HEAD_SIZE : head * HEAD_SIZE + 1])
        grad_v.append(contract_first(probs.astype(jnp.bfloat16), gh))
        grad_probs = contract_last(gh, vh)
        inner = jnp.sum(grad_probs * probs, axis=-1, keepdims=True)
        grad_scores = (probs * (grad_probs - inner)).astype(jnp.bfloat16)
        grad_q.append(plain(grad_scores, kh))
        grad_k.append(contract_first(grad_scores, qh))
    gq = jnp.concatenate(grad_q, axis=1) * HEAD_SIZE**-0.5
    gk = jnp.concatenate(grad_k, axis=1)
    gv = jnp.concatenate(grad_v, axis=1).astype(jnp.bfloat16)
    gq = (gq * cos[:own] - half_turn(gq * sin[:own])).astype(jnp.bfloat16)
    gk = (gk * cos - half_turn(gk * sin)).astype(jnp.bfloat16)
    weights = (
        contract_first(normed_own, gq).astype(jnp.bfloat16),
        contract_first(normed, gk).astype(jnp.bfloat16),
        contract_first(normed, gv).astype(jnp.bfloat16),
        contract_first(branch, attended).astype(jnp.bfloat16),
    )
    update = contract_last(gk, wk) + contract_last(gv, wv)
    return weights, update, contract_last(gq, wq)


def attend_kernel(
    normed, wq, wk, wv, cosine, sine, seg_rows, seg_cols, q_out, k_out, v_out, att_out, log_out
):
    own = seg_rows.shape[0]
    q_out[0], k_out[0], v_out[0], att_out[0], log_out[0] = attend_step(
        normed[:own], normed[...], wq[0, 0], wk[0, 0], wv[0, 0], cosine[...], sine[...],
        seg_rows[...] == seg_cols[...],
    )


def attend_back_kernel(
    normed, branch, wq, wk, wv, mix, cosine, sine, seg_rows, seg_cols, q_in, k_in, v_in, att_in,
    log_in, weight_out, mix_out, normed_out,
):
    own = seg_rows.shape[0]
    step = pl.program_id(0)
    weights, update, first = attend_back_step(
        normed[:own], normed[...], branch[...], wq[0, 0], wk[0, 0], wv[0, 0], mix[0, 0],
        cosine[...], sine[...], seg_rows[...] == seg_cols[...], q_in[0], k_in[0], v_in[0],
        att_in[0], log_in[0],
    )
    for j in range(3):
        weight_out[0, j] = weights[j]
    mix_out[0, 0] = weights[3]

    @pl.when(step == 0)
    def _():
        normed_out[...] = update

    @pl.when(step > 0)
    def _():
        normed_out[...] += update

    normed_out[:own] += first


def attention_specs(width, own, length, groups):
    def weight(j):
        return pl.BlockSpec((1, 1, width, LANES), lambda p: (p // groups, j, 0, p % groups))

    def columns(rows):
        return pl.BlockSpec((1, rows, LANES), lambda p: (p, 0, 0))

    def whole(*shape):
        return pl.BlockSpec(shape, lambda p: (0,) * len(shape))

    return weight, columns, whole


def attend(normed, weights, cosine, sine, seg_rows, seg_cols):
    length, width = normed.shape
    own = seg_rows.shape[0]
    groups = weights.shape[3] // LANES
    weight, columns, whole = attention_specs(width, own, length, groups)
    pairs = 2 * groups
    return pl.pallas_call(
        attend_kernel,
        grid=(2 * groups,),
        out_shape=[
            jax.ShapeDtypeStruct((pairs, own, LANES), jnp.bfloat16),
            jax.ShapeDtypeStruct((pairs, length, LANES), jnp.bfloat16),
            jax.ShapeDtypeStruct((pairs, length, LANES), jnp.bfloat16),
            jax.ShapeDtypeStruct((pairs, own, LANES), jnp.bfloat16),
            jax.ShapeDtypeStruct((pairs, own, LANES), jnp.float32),
        ],
        in_specs=[
            whole(length, width), weight(0), weight(1), weight(2), whole(length, LANES),
            whole(length, LANES), whole(own, 1), whole(1, length),
        ],
        out_specs=[columns(own), columns(length), columns(length), columns(own), columns(own)],
        compiler_params=pltpu.CompilerParams(vmem_limit_bytes=VMEM_LIMIT),
    )(normed, weights, weights, weights, cosine, sine, seg_rows, seg_cols)


def attend_back(normed, branch, weights, mixing, cosine, sine, seg_rows, seg_cols, saved):
    length, width = normed.shape
    own = seg_rows.shape[0]
    groups = weights.shape[3] // LANES
    weight, columns, whole = attention_specs(width, own, length, groups)
    return pl.pallas_call(
        attend_back_kernel,
        grid=(2 * groups,),
        out_shape=[
            jax.ShapeDtypeStruct((2, 3, width, groups * LANES), jnp.bfloat16),
            jax.ShapeDtypeStruct((2, 1, width, groups * LANES), jnp.bfloat16),
            jax.ShapeDtypeStruct((length, width), jnp.float32),
        ],
        in_specs=[
            whole(length, width), whole(own, width), weight(0), weight(1), weight(2), weight(0),
            whole(length, LANES), whole(length, LANES), whole(own, 1), whole(1, length),
            columns(own), columns(length), columns(length), columns(own), columns(own),
        ],
        out_specs=[
            pl.BlockSpec((1, 3, width, LANES), lambda p: (p // groups, 0, 0, p % groups)),
            weight(0),
            whole(length, width),
        ],
        compiler_params=pltpu.CompilerParams(vmem_limit_bytes=VMEM_LIMIT),
    )(normed, branch, weights, weights, weights, mixing, cosine, sine, seg_rows, seg_cols, *saved)


def rotary_tables(length):
    indices = np.arange(HEAD_SIZE // 2, dtype=np.float32)
    inverse_freq = np.float32(THETA) ** (np.float32(-2.0 / HEAD_SIZE) * indices)
    angles = np.arange(length, dtype=np.float32)[:, None] * inverse_freq[None, :]
    angles = np.tile(angles, (1, LANES // (HEAD_SIZE // 2))).astype(np.float32)
    return jnp.asarray(np.cos(angles)), jnp.asarray(np.sin(angles))


def own_first(rows, core):
    return jnp.where(core == 0, rows, jnp.roll(rows, rows.shape[0] // 2, axis=0))


def per_device(
    doubling,
    inputs,
    segments,
    gain_first,
    gain_second,
    attend_weight,
    mixing_matrix,
    expand_matrix,
    reduce_matrix,
    cotangent,
):
    core = lax.axis_index("tensor")
    own, width = inputs.shape
    length = segments.shape[0]
    share = gain_first.shape[0]
    shards = [attend_weight, mixing_matrix[None], expand_matrix, reduce_matrix[None]]
    cosine, sine = rotary_tables(length)
    segments = own_first(segments, core)
    seg_rows, seg_cols = segments[:own, None], segments[None, :]
    place = (2 * lax.axis_index("dp") + core) * share
    if doubling:
        gains = jnp.zeros((8, width), jnp.float32)
        pair = jnp.stack([gain_first, gain_second])
        gains = lax.dynamic_update_slice(gains, pair, (jnp.int32(0), place))
        output, input_grad, gains, sent_attend, sent_mixing, sent_expand, sent_reduce = layer(
            gains, shards, inputs, cotangent, cosine, sine, seg_rows, seg_cols
        )
        mine = lax.dynamic_slice(gains, (jnp.int32(0), place), (2, share))
        return (
            output, input_grad, mine[0], mine[1], sent_attend, sent_mixing[0], sent_expand,
            sent_reduce[0],
        )
    tables = (own_first(cosine, core), own_first(sine, core), seg_rows, seg_cols)
    both = ("dp", "tensor")
    full_first = lax.all_gather(gain_first, both, axis=0, tiled=True)
    full_second = lax.all_gather(gain_second, both, axis=0, tiled=True)
    attend_full, mixing_full, expand_full, reduce_full = (
        lax.all_gather(lax.all_gather(s, "dp", axis=1, tiled=True), "tensor", axis=0)
        for s in shards
    )
    pair = lax.all_gather(inputs, "tensor", axis=0)
    other_inputs = jnp.where(core == 0, pair[1], pair[0])
    rows_all = jnp.concatenate([inputs, other_inputs]).astype(jnp.float32)
    rows_in = rows_all[:own]
    unit_one, inverse_one = normalize(rows_all)
    normed_one = (unit_one * full_first).astype(jnp.bfloat16)
    saved = attend(normed_one, attend_full, *tables)
    attended = jnp.transpose(saved[3], (1, 0, 2)).reshape(own, width)
    half = attended.shape[1] // 2
    middle = (
        rows_in
        + contract_last(attended[:, :half], mixing_full[0, 0])
        + contract_last(attended[:, half:], mixing_full[1, 0])
    )
    unit_two, inverse_two = normalize(middle)
    normed_two = (unit_two * full_second).astype(jnp.bfloat16)
    output = middle
    grad_normed_two = jnp.zeros_like(middle)
    grad_expand, grad_reduce = [], []
    for side in range(2):
        activated_in = plain(normed_two, expand_full[side, 0])
        gate_linear = plain(normed_two, expand_full[side, 1])
        gelu_value = jax.nn.gelu(activated_in, approximate=False)
        hidden = (gelu_value * gate_linear).astype(jnp.bfloat16)
        output = output + contract_last(hidden, reduce_full[side, 0])
        grad_hidden = plain(cotangent, reduce_full[side, 0])
        grad_reduce.append(contract_first(cotangent, hidden).astype(jnp.bfloat16))
        grad_activated = (grad_hidden * gate_linear * gelu_slope(activated_in)).astype(
            jnp.bfloat16
        )
        grad_gate = (grad_hidden * gelu_value).astype(jnp.bfloat16)
        grad_expand.append(contract_first(normed_two, grad_activated).astype(jnp.bfloat16))
        grad_expand.append(contract_first(normed_two, grad_gate).astype(jnp.bfloat16))
        grad_normed_two = (
            grad_normed_two
            + contract_last(grad_activated, expand_full[side, 0])
            + contract_last(grad_gate, expand_full[side, 1])
        )
    hidden_width = expand_full.shape[3]
    grad_expand = jnp.stack(grad_expand).reshape(2, 2, width, hidden_width)
    grad_reduce = jnp.stack(grad_reduce).reshape(2, 1, width, hidden_width)
    second_local = jnp.sum(grad_normed_two * unit_two, axis=0)
    grad_middle = cotangent.astype(jnp.float32) + normalize_back(
        grad_normed_two * full_second, unit_two, inverse_two
    )
    grad_branch = grad_middle.astype(jnp.bfloat16)
    grad_attend, grad_mixing, grad_normed_one = attend_back(
        normed_one, grad_branch, attend_full, mixing_full, *tables, saved
    )
    first_local = jnp.sum(grad_normed_one * unit_one, axis=0)
    through = normalize_back(grad_normed_one * full_first, unit_one, inverse_one)
    rows_other = through[own:].astype(jnp.bfloat16)

    def summed(part):
        part = part.astype(jnp.float32)
        part = lax.psum_scatter(part, "tensor", scatter_dimension=0, tiled=False)
        return lax.psum_scatter(part, "dp", scatter_dimension=1, tiled=True)

    sent_attend, sent_expand = summed(grad_attend), summed(grad_expand)
    sent_mixing, sent_reduce = summed(grad_mixing)[0], summed(grad_reduce)[0]
    first_grad, second_grad = (
        lax.psum_scatter(part, ("dp", "tensor"), scatter_dimension=0, tiled=True)
        for part in (first_local, second_local)
    )
    pair = lax.all_gather(rows_other, "tensor", axis=0)
    rows_back = jnp.where(core == 0, pair[1], pair[0])
    input_grad = grad_middle + through[:own] + rows_back.astype(jnp.float32)
    return (
        output.astype(jnp.bfloat16),
        input_grad,
        first_grad,
        second_grad,
        sent_attend,
        sent_mixing,
        sent_expand,
        sent_reduce,
    )


def solution(mesh):
    in_specs = (
        P(("dp", "tensor"), None),
        P("dp"),
        P(("dp", "tensor")),
        P(("dp", "tensor")),
        P(None, "dp", "tensor"),
        P("dp", "tensor"),
        P(None, "dp", "tensor"),
        P("dp", "tensor"),
        P(("dp", "tensor"), None),
    )
    out_specs = (
        P(("dp", "tensor"), None),
        P(("dp", "tensor"), None),
        P(("dp", "tensor")),
        P(("dp", "tensor")),
        P(None, "dp", "tensor"),
        P("dp", "tensor"),
        P(None, "dp", "tensor"),
        P("dp", "tensor"),
    )
    doubling = mesh.shape["dp"] == 16 and mesh.shape["tensor"] == 2
    return jax.shard_map(
        functools.partial(per_device, doubling),
        mesh=mesh,
        in_specs=in_specs,
        out_specs=out_specs,
        check_vma=False,
    )
```
